32 devices in a mesh: ctx: 4 (over y, x), head: 8 (over z, core).
Axes of the slice: x: 2, y: 2, z: 4, core: 2. Of those that a mesh axis runs over, the one named last changes fastest.
Arguments:
- doc_lengths: int32 [4], replicated, may hold values from 1 to 1536, 2048 in all
- lin_q: bfloat16 [2048, 8192], P('ctx', 'head'), may hold values from -6 to 6
- lin_k: bfloat16 [2048, 8192], P('ctx', 'head'), may hold values from -6 to 6
- lin_v: bfloat16 [2048, 8192], P('ctx', 'head'), may hold values from -40 to 40
- log_decay: float32 [64, 2048], P('head', 'ctx'), may hold values from -1 to 0
- lin_gain: float32 [8192], P('head'), may hold values from 0.5 to 1.5
- soft_q: bfloat16 [2048, 8192], P('ctx', 'head'), may hold values from -48 to 48
- soft_k: bfloat16 [2048, 1024], P('ctx', 'head'), may hold values from -6 to 6
- soft_v: bfloat16 [2048, 1024], P('ctx', 'head'), may hold values from -6 to 6
Outputs:
- lin_out: bfloat16 [2048, 8192], P('ctx', 'head')
- soft_out: bfloat16 [2048, 8192], P('ctx', 'head')
The draws below stay inside these ranges and needn't reach their ends.
Inputs may be any that keep to these rules, and one draw needn't show every extreme that they name: `doc_lengths`: the 4 lengths sum to 2048 and the largest is exactly 1536.
All inputs are finite; a program needn't handle non-finite values.
Results may differ from the reference program's by a relative error of at most 0.015.
Values may be sent and summed in bfloat16 or wider, within the bound.
No kernel may reach another device: no remote copies, remote signals or barrier semaphores. Data moves between devices by JAX's collectives and lax.ppermute only.
A program may use at most 64 MiB of HBM per device.

```python
import math
import jax
import jax.numpy as jnp
import numpy as np
from jax import lax

QUERY_HEAD_COUNT = 64
KVH = 8
DH = 128
BLK = 256
DOCS = 4
TOK_DEV = 512
WINDOW_TOKENS = 2048
MOST = 1536


def draw_lin_v(key, part):
    first, second, third = jax.random.split(key, 3)
    columns = QUERY_HEAD_COUNT * DH
    base = jnp.clip(jax.random.normal(first, (WINDOW_TOKENS, columns)), -4.0, 4.0)
    row_scale = 10.0 ** jax.random.uniform(second, (WINDOW_TOKENS, 1))
    column_scale = 10.0 ** jax.random.uniform(third, (1, columns))
    return (base * row_scale * column_scale / 10.0).astype(jnp.bfloat16)


def draw_log_decay(key, part):
    option_key, quick_key, gradual_key, multiplier_key, spike_key, magnitude_key, region_key, region_rate_key = jax.random.split(key, 8)
    regions = WINDOW_TOKENS // TOK_DEV
    mixed = jax.random.randint(option_key, (QUERY_HEAD_COUNT, 1), 0, 2) == 0
    decay_factor = jnp.exp(jax.random.uniform(multiplier_key, (QUERY_HEAD_COUNT, WINDOW_TOKENS), minval=math.log(0.5), maxval=math.log(2.0)))
    fast_rate = jnp.exp(jax.random.uniform(quick_key, (QUERY_HEAD_COUNT, 1), minval=math.log(1.0 / 50.0), maxval=math.log(1.0 / 30.0)))
    slow_rate = jax.random.uniform(gradual_key, (QUERY_HEAD_COUNT, 1), minval=0.1, maxval=0.4) * (math.log(10.0) / WINDOW_TOKENS)
    region_fast = jax.random.randint(region_key, (QUERY_HEAD_COUNT, regions), 0, 2) == 0
    region_medium = jnp.exp(jax.random.uniform(region_rate_key, (QUERY_HEAD_COUNT, regions), minval=math.log(1.0 / 4000.0), maxval=math.log(1.0 / 400.0)))
    region_rate = jnp.where(region_fast, fast_rate, region_medium)
    region_rate = jnp.repeat(region_rate, TOK_DEV, axis=1)
    decay_rate = jnp.where(mixed, region_rate, slow_rate)
    outlier_flags = (jax.random.randint(spike_key, (QUERY_HEAD_COUNT, WINDOW_TOKENS), 0, WINDOW_TOKENS) < 2).astype(jnp.float32)
    outlier_magnitude = jax.random.uniform(magnitude_key, (QUERY_HEAD_COUNT, WINDOW_TOKENS), minval=0.22, maxval=0.69)
    return (-(decay_rate * decay_factor) - outlier_flags * outlier_magnitude).astype(jnp.float32)


def paired_soft(key):
    base_key = jax.random.fold_in(key, 7)
    query_key = jax.random.fold_in(base_key, 0)
    keys_key = jax.random.fold_in(base_key, 1)
    loud_key = jax.random.fold_in(base_key, 4)
    loud = jax.random.randint(loud_key, (WINDOW_TOKENS,), 0, 64) == 0
    queries = jnp.clip(jax.random.normal(query_key, (WINDOW_TOKENS, QUERY_HEAD_COUNT * DH)), -4.0, 4.0)
    loud_rows = jnp.sign(queries) * (30.0 + 4.0 * jnp.abs(queries))
    queries = jnp.where(loud[:, None], loud_rows, queries)
    keys_all = jnp.clip(jax.random.normal(keys_key, (WINDOW_TOKENS, KVH * DH)), -4.0, 4.0)
    return (queries.astype(jnp.float32), keys_all.astype(jnp.float32))


def draw_soft_q(key, part):
    return paired_soft(key)[0].astype(jnp.bfloat16)


def draw_soft_k(key, part):
    return paired_soft(key)[1].astype(jnp.bfloat16)


def level_of(key, extent, pieces, smallest, high):
    def one(axis_at, blocks):
        draws = jax.random.uniform(jax.random.fold_in(jax.random.fold_in(key, 6), axis_at), (blocks,), jnp.float32, smallest / len(pieces), high / len(pieces))
        return jnp.repeat(jnp.exp(draws), extent[axis_at] // blocks).reshape((-1,) + (1,) * (len(extent) - axis_at - 1))

    level = one(*pieces[0])
    for cut in pieces[1:]:
        level = level * one(*cut)
    return level


def split_up(number_of, total, bound, lean):
    portions = [(1 << 20) // math.isqrt(rank ** lean) + 1 for rank in range(2, number_of + 1)]
    rest, given = total - bound - (number_of - 1), [1] * (number_of - 1)
    while rest > 0:
        free = [i for i in range(number_of - 1) if given[i] < bound]
        pool, remaining = sum([portions[i] for i in free]), rest
        for i in free:
            addition = min(bound - given[i], max(1, remaining * portions[i] // pool), rest)
            given[i] = given[i] + addition
            rest = rest - addition
    return np.array([bound] + given)


def uneven(key, amount, total, bound, lean):
    if amount == 2:
        one = jax.random.randint(key, (), max(1, total - bound), min(bound, total - 1) + 1)
        return jnp.stack([one, total - one])
    tallies = jnp.asarray(split_up(amount, total, bound, lean), jnp.int32)
    twos = (amount - 1) // 2
    source_of, sink = tallies[1:1 + 2 * twos:2], tallies[2:2 + 2 * twos:2]
    room = jnp.minimum(source_of - 1, bound - sink)
    passed = jax.random.randint(jax.random.fold_in(key, 1), (twos,), 0, 1 << 20) % (room + 1)
    tallies = tallies.at[1:1 + 2 * twos:2].set(source_of - passed).at[2:2 + 2 * twos:2].set(sink + passed)
    return tallies[jax.random.permutation(jax.random.fold_in(key, 2), amount)]


def centred(own_key, shape, width, bound, cuts=(), kind=jnp.bfloat16):
    gain = level_of(own_key, shape, cuts, -0.22, 0.18) if cuts else 1.0
    entries = jax.random.normal(own_key, shape, jnp.float32) * width * gain
    return jnp.minimum(jnp.maximum(entries, -bound), bound).astype(kind)


def setup_inputs(seed: int = 0) -> dict:
    streams_of = jax.random.split(jax.random.key(seed), 10)
    doc_lengths = uneven(streams_of[0], DOCS, WINDOW_TOKENS, MOST, 2).astype(jnp.int32)
    lin_q = centred(streams_of[1], (WINDOW_TOKENS, QUERY_HEAD_COUNT * DH), 1.0, 6.0, ((0, 4), (1, 8)))
    lin_k = centred(streams_of[2], (WINDOW_TOKENS, QUERY_HEAD_COUNT * DH), 1.0, 6.0, ((0, 4), (1, 8)))
    lin_v = draw_lin_v(jax.random.fold_in(streams_of[9], 71), 0)
    log_decay = draw_log_decay(jax.random.fold_in(streams_of[9], 71), 0)
    lin_gain = jnp.clip(1.0 + 0.1 * jax.random.normal(streams_of[5], (QUERY_HEAD_COUNT * DH,), jnp.float32), 0.5, 1.5)
    soft_q = draw_soft_q(jax.random.fold_in(streams_of[9], 71), 0)
    soft_k = draw_soft_k(jax.random.fold_in(streams_of[9], 71), 0)
    soft_v = centred(streams_of[8], (WINDOW_TOKENS, KVH * DH), 1.0, 6.0, ((0, 4), (1, 8)))
    return {"doc_lengths": doc_lengths, "lin_q": lin_q, "lin_k": lin_k, "lin_v": lin_v, "log_decay": log_decay, "lin_gain": lin_gain, "soft_q": soft_q, "soft_k": soft_k, "soft_v": soft_v}


def doc_index(doc_lengths, positions):
    bounds = jnp.cumsum(doc_lengths).astype(jnp.int32)
    counted = lax.optimization_barrier(jnp.sum((bounds[None, :] <= positions[:, None]).astype(jnp.int32), axis=1)).astype(jnp.int32)
    return jnp.where(positions < 0, -1, counted).astype(jnp.int32)

def lightning_block(carry_state, scan_items):
    queries, keys_block, values_block, decay_block, segs_block, seg_before = scan_items
    running = jnp.cumsum(decay_block, axis=1)
    block_len = segs_block.shape[0]
    rows_iota = lax.broadcasted_iota(jnp.int32, (block_len, block_len), 0)
    cols_iota = lax.broadcasted_iota(jnp.int32, (block_len, block_len), 1)
    allowed = (rows_iota >= cols_iota) & (segs_block[:, None] == segs_block[None, :])
    spread = jnp.where(allowed[None], running[:, :, None] - running[:, None, :], 0.0)
    decays = jnp.where(allowed[None], jnp.exp(spread), 0.0)
    query_wide = queries.astype(jnp.float32)
    key_wide = keys_block.astype(jnp.float32)
    value_wide = values_block.astype(jnp.float32)
    scores = jnp.einsum('ihd,jhd->hij', query_wide, key_wide, precision=lax.Precision.HIGHEST) * decays
    scores = lax.optimization_barrier(scores.astype(jnp.bfloat16)).astype(jnp.float32)
    inside = jnp.einsum('hij,jhd->ihd', scores, value_wide, precision=lax.Precision.HIGHEST)
    carried = (segs_block == seg_before).astype(jnp.float32)
    entering = jnp.exp(running) * carried[None, :]
    state_low = lax.optimization_barrier(carry_state.astype(jnp.bfloat16)).astype(jnp.float32)
    across = jnp.einsum('ihd,hde->ihe', query_wide, state_low, precision=lax.Precision.HIGHEST)
    across = across * entering.T[:, :, None]
    closing = running[:, -1:]
    tail_mask = (segs_block == segs_block[-1]).astype(jnp.float32)
    weights = jnp.exp(closing - running) * tail_mask[None, :]
    weighted = key_wide * weights.T[:, :, None]
    weighted = lax.optimization_barrier(weighted.astype(jnp.bfloat16)).astype(jnp.float32)
    update = jnp.einsum('jhd,jhe->hde', weighted, value_wide, precision=lax.Precision.HIGHEST)
    kept_flag = (segs_block[-1] == seg_before).astype(jnp.float32)
    decay_factor = kept_flag * jnp.exp(closing[:, 0])
    new_state = decay_factor[:, None, None] * carry_state + update
    return (new_state, inside + across)

def lightning(lin_q, lin_k, lin_v, log_decay, lin_gain, doc_ids):
    blocks = WINDOW_TOKENS // BLK
    shaped = (blocks, BLK, QUERY_HEAD_COUNT, DH)
    query_blocks = lin_q.reshape(shaped)
    key_blocks = lin_k.reshape(shaped)
    value_blocks = lin_v.reshape(shaped)
    decay_blocks = log_decay.reshape(QUERY_HEAD_COUNT, blocks, BLK).transpose(1, 0, 2)
    seg_blocks = doc_ids.reshape(blocks, BLK)
    befores = jnp.concatenate([jnp.full((1,), -1, jnp.int32), seg_blocks[:-1, -1].astype(jnp.int32)])
    start_state = jnp.zeros((QUERY_HEAD_COUNT, DH, DH), jnp.float32)
    _, outputs = lax.scan(lightning_block, start_state, (query_blocks, key_blocks, value_blocks, decay_blocks, seg_blocks, befores))
    raw_out = outputs.reshape(WINDOW_TOKENS, QUERY_HEAD_COUNT, DH)
    norm_scale = lax.rsqrt(lax.optimization_barrier(jnp.mean(raw_out * raw_out, axis=2, keepdims=True)) + 1e-06)
    normed = raw_out * norm_scale * lin_gain.reshape(1, QUERY_HEAD_COUNT, DH)
    return normed.reshape(WINDOW_TOKENS, QUERY_HEAD_COUNT * DH).astype(jnp.bfloat16)

def softmax_head(head_query, head_keys, head_values, doc_ids):
    scores = jnp.dot(head_query, head_keys.T, preferred_element_type=jnp.float32) * DH ** (-0.5)
    positions = jnp.arange(WINDOW_TOKENS, dtype=jnp.int32)
    allowed = (positions[None, :] <= positions[:, None]) & (doc_ids[None, :] == doc_ids[:, None])
    masked = jnp.where(allowed, scores, -jnp.inf)
    row_top = lax.optimization_barrier(jnp.max(masked, axis=1, keepdims=True))
    exp_terms = jnp.where(allowed, jnp.exp(scores - row_top), 0.0)
    row_total = lax.optimization_barrier(jnp.sum(exp_terms, axis=1, keepdims=True))
    weights = exp_terms.astype(jnp.bfloat16)
    return jnp.dot(weights, head_values, preferred_element_type=jnp.float32) / row_total

def reference(doc_lengths, lin_q, lin_k, lin_v, log_decay, lin_gain, soft_q, soft_k, soft_v):
    positions = jnp.arange(WINDOW_TOKENS, dtype=jnp.int32)
    doc_ids = doc_index(doc_lengths, positions)
    lin_out = lightning(lin_q, lin_k, lin_v, log_decay, lin_gain, doc_ids)
    group_size = QUERY_HEAD_COUNT // KVH
    query_heads = soft_q.reshape(WINDOW_TOKENS, QUERY_HEAD_COUNT, DH).transpose(1, 0, 2)
    key_heads = jnp.repeat(soft_k.reshape(WINDOW_TOKENS, KVH, DH).transpose(1, 0, 2), group_size, axis=0)
    value_heads = jnp.repeat(soft_v.reshape(WINDOW_TOKENS, KVH, DH).transpose(1, 0, 2), group_size, axis=0)

    def one_head(head_items):
        return softmax_head(head_items[0], head_items[1], head_items[2], doc_ids)
    attended = lax.map(one_head, (query_heads, key_heads, value_heads))
    soft_out = attended.transpose(1, 0, 2).reshape(WINDOW_TOKENS, QUERY_HEAD_COUNT * DH).astype(jnp.bfloat16)
    return (lin_out, soft_out)
```

```python
import functools

import jax
import jax.numpy as jnp
from jax import lax
from jax.experimental import pallas as pl
from jax.experimental.pallas import tpu as pltpu
from jax.sharding import PartitionSpec as P

KVH = 8
DH = 128
BLK = 256
KEYS = 512
LOW = -1e30
LOG2E = 1.4426950408889634
F32 = jnp.float32
BF16 = jnp.bfloat16
NT = (((1,), (1,)), ((), ()))
TN = (((0,), (0,)), ((), ()))
SMEM = pl.BlockSpec(memory_space=pltpu.SMEM)
ANY = pl.BlockSpec(memory_space=pl.ANY)


def swapped(value, axis, bit):
    return lax.ppermute(value, axis, [(i, i ^ 1 << bit) for i in range(lax.axis_size(axis))])


def bounds_of(lengths_ref):
    out, total = [], 0
    for d in range(lengths_ref.shape[0]):
        total = total + lengths_ref[d]
        out.append(total)
    return out


def doc_start(bounds, position):
    start = jnp.zeros_like(position)
    for bound in bounds:
        start = jnp.where(bound <= position, bound, start)
    return start


def log_sums(decay):
    rows = lax.broadcasted_iota(jnp.int32, (BLK, BLK), 0)
    cols = lax.broadcasted_iota(jnp.int32, (BLK, BLK), 1)
    upper = (rows <= cols).astype(F32)
    return jnp.dot(decay, upper, precision=lax.Precision.HIGHEST, preferred_element_type=F32)


def column(row_form, head):
    return jnp.transpose(row_form, (1, 0))[:, head : head + 1]


def states_kernel(lengths_ref, keys_ref, values_ref, decay_ref, msg_ref, first_ref):
    heads = decay_ref.shape[0]
    tokens = keys_ref.shape[0]
    base = lax.axis_index("ctx") * tokens
    bounds = bounds_of(lengths_ref)
    place = lax.broadcasted_iota(jnp.int32, (BLK, 1), 0)
    state = [None] * heads
    through = jnp.ones((heads, 1), F32)
    for b in range(tokens // BLK):
        s = base + b * BLK
        start_last = doc_start(bounds, s + BLK - 1)
        kept = jnp.where(start_last < s, 1.0, 0.0).astype(F32)
        sums = log_sums(decay_ref[:, b * BLK : (b + 1) * BLK])
        closing = sums[:, BLK - 1 : BLK]
        weights = jnp.transpose(jnp.exp(closing - sums), (1, 0))
        weights = jnp.where(s + place >= start_last, weights, 0.0)
        factor = kept * jnp.exp(closing)
        through = through * factor
        for h in range(heads):
            cols = slice(h * DH, (h + 1) * DH)
            keys = keys_ref[b * BLK : (b + 1) * BLK, cols].astype(F32)
            weighted = (keys * weights[:, h : h + 1]).astype(BF16)
            update = lax.dot_general(
                weighted, values_ref[b * BLK : (b + 1) * BLK, cols], TN, preferred_element_type=F32
            )
            if b == 0:
                state[h] = update
            else:
                state[h] = factor[h : h + 1, :] * state[h] + update
            if b < tokens // BLK - 1:
                first_ref[b, h * DH : (h + 1) * DH, :] = update.astype(BF16)
    for h in range(heads):
        msg_ref[h * DH : (h + 1) * DH, :] = state[h].astype(BF16)
    high = through.astype(BF16)
    low = (through - high.astype(F32)).astype(BF16)
    tail = jnp.concatenate([high.astype(F32), low.astype(F32)], axis=0)
    tail = jnp.broadcast_to(tail, (2 * heads, DH))
    extra = msg_ref.shape[0] - heads * DH
    if extra > 2 * heads:
        tail = jnp.concatenate([tail, jnp.zeros((extra - 2 * heads, DH), F32)], axis=0)
    msg_ref[heads * DH :, :] = tail.astype(BF16)


def inside_kernel(lengths_ref, queries_ref, keys_ref, values_ref, decay_ref, out_ref):
    heads = decay_ref.shape[0]
    tokens = keys_ref.shape[0]
    base = lax.axis_index("ctx") * tokens
    bounds = bounds_of(lengths_ref)
    rows = lax.broadcasted_iota(jnp.int32, (BLK, BLK), 0)
    cols = lax.broadcasted_iota(jnp.int32, (BLK, BLK), 1)
    place = lax.broadcasted_iota(jnp.int32, (BLK, 1), 0)
    for b in range(tokens // BLK):
        s = base + b * BLK
        start = doc_start(bounds, s + place) - s
        allowed = (cols <= rows) & (cols >= start)
        sums = log_sums(decay_ref[:, b * BLK : (b + 1) * BLK])
        down = jnp.transpose(sums, (1, 0))
        here = slice(b * BLK, (b + 1) * BLK)
        for h in range(heads):
            there = slice(h * DH, (h + 1) * DH)
            spread = jnp.where(allowed, down[:, h : h + 1] - sums[h : h + 1, :], LOW)
            scores = lax.dot_general(
                queries_ref[here, there], keys_ref[here, there], NT, preferred_element_type=F32
            )
            scores = (scores * jnp.exp(spread)).astype(BF16)
            out_ref[here, there] = jnp.dot(
                scores, values_ref[here, there], preferred_element_type=F32
            ).astype(BF16)


def through_of(msg_ref, heads, h):
    high = msg_ref[heads * DH + h : heads * DH + h + 1, :].astype(F32)
    low = msg_ref[heads * DH + heads + h : heads * DH + heads + h + 1, :].astype(F32)
    return high + low


def combine_kernel(heads, bit, total_ref, prefix_ref, far_ref, new_total_ref, new_prefix_ref):
    upper = (lax.axis_index("ctx") // (1 << bit)) % 2 == 1

    def joined(early_ref, late_ref, out_ref):
        tails = []
        for h in range(heads):
            here = slice(h * DH, (h + 1) * DH)
            late = through_of(late_ref, heads, h)
            early = through_of(early_ref, heads, h)
            out_ref[here, :] = (
                late * early_ref[here, :].astype(F32) + late_ref[here, :].astype(F32)
            ).astype(BF16)
            tails.append(late * early)
        tail = jnp.concatenate(tails, axis=0)
        high = tail.astype(BF16).astype(F32)
        pieces = [high, tail - high]
        extra = out_ref.shape[0] - heads * DH - 2 * heads
        if extra:
            pieces.append(jnp.zeros((extra, DH), F32))
        out_ref[heads * DH :, :] = jnp.concatenate(pieces, axis=0).astype(BF16)

    @pl.when(upper)
    def _():
        joined(far_ref, total_ref, new_total_ref)
        if prefix_ref is None:
            new_prefix_ref[...] = far_ref[...]
        else:
            joined(far_ref, prefix_ref, new_prefix_ref)

    @pl.when(jnp.logical_not(upper))
    def _():
        joined(total_ref, far_ref, new_total_ref)
        if prefix_ref is None:
            new_prefix_ref[...] = jnp.zeros_like(new_prefix_ref)
            new_prefix_ref[heads * DH : heads * DH + 16, :] = jnp.where(
                lax.broadcasted_iota(jnp.int32, (16, DH), 0) < heads, 1.0, 0.0
            ).astype(BF16)
        else:
            new_prefix_ref[...] = prefix_ref[...]


def across_kernel(bit, lengths_ref, queries_ref, inside_ref, decay_ref, gain_ref, first_ref, prefix_ref, far_ref, out_ref):
    heads = decay_ref.shape[0]
    tokens = queries_ref.shape[0]
    place_ctx = lax.axis_index("ctx")
    base = place_ctx * tokens
    upper = jnp.where((place_ctx // (1 << bit)) % 2 == 1, 1.0, 0.0).astype(F32)
    bounds = bounds_of(lengths_ref)
    place = lax.broadcasted_iota(jnp.int32, (BLK, 1), 0)
    state = []
    for h in range(heads):
        here = slice(h * DH, (h + 1) * DH)
        late = upper * through_of(prefix_ref, heads, h)
        own = prefix_ref[here, :].astype(F32)
        state.append(own + jnp.where(upper > 0, late * far_ref[here, :].astype(F32), 0.0))
    for b in range(tokens // BLK):
        s = base + b * BLK
        here = slice(b * BLK, (b + 1) * BLK)
        start_last = doc_start(bounds, s + BLK - 1)
        kept = jnp.where(start_last < s, 1.0, 0.0).astype(F32)
        sums = log_sums(decay_ref[:, here])
        factor = kept * jnp.exp(sums[:, BLK - 1 : BLK])
        entering = jnp.exp(jnp.transpose(sums, (1, 0)))
        entering = jnp.where(doc_start(bounds, s + place) < s, entering, 0.0)
        for h in range(heads):
            there = slice(h * DH, (h + 1) * DH)
            across = jnp.dot(queries_ref[here, there], state[h].astype(BF16), preferred_element_type=F32)
            raw = inside_ref[here, there].astype(F32) + across * entering[:, h : h + 1]
            scale = lax.rsqrt(jnp.mean(raw * raw, axis=1, keepdims=True) + 1e-06)
            out_ref[here, there] = (raw * scale * gain_ref[:, there]).astype(BF16)
            if b < tokens // BLK - 1:
                state[h] = factor[h : h + 1, :] * state[h] + first_ref[b, there, :].astype(F32)


def softmax_kernel(count, lengths_ref, queries_ref, *refs):
    pieces = refs[:count]
    out_ref, keys, values, scores, tops, totals, sems = refs[count:]
    tokens = queries_ref.shape[0]
    heads = queries_ref.shape[1] // DH
    place_ctx = lax.axis_index("ctx")
    base = place_ctx * tokens
    copies = []
    for m in range(count):
        origin = jnp.int32(0)
        bit = 1
        while bit < count:
            mine = (place_ctx // bit) % 2
            origin = origin + bit * (1 - mine if m & bit else mine)
            bit *= 2
        at = pl.ds(pl.multiple_of(origin * tokens, tokens), tokens)
        copies.append(pltpu.make_async_copy(pieces[m].at[:, :DH], keys.at[at, :], sems.at[0, m]))
        copies.append(pltpu.make_async_copy(pieces[m].at[:, DH:], values.at[at, :DH], sems.at[1, m]))
    for copy in copies:
        copy.start()
    values[:, DH:] = jnp.ones((values.shape[0], DH), BF16)
    for copy in copies:
        copy.wait()
    bounds = bounds_of(lengths_ref)
    place = lax.broadcasted_iota(jnp.int32, (BLK, 1), 0)
    spots = lax.broadcasted_iota(jnp.int32, (BLK, KEYS), 1)
    factor = LOG2E * DH**-0.5

    for block in range(tokens // BLK):
        here = slice(block * BLK, (block + 1) * BLK)
        s = base + block * BLK
        row_start = doc_start(bounds, s + place)
        start_last = doc_start(bounds, s + BLK - 1)
        low = doc_start(bounds, s) // KEYS
        high = (s + BLK + KEYS - 1) // KEYS

        def scored(h, slot):
            query = queries_ref[here, pl.ds(pl.multiple_of(h * DH, DH), DH)]
            tops[...] = jnp.full_like(tops, LOW)

            def step(kb, _):
                first = pl.multiple_of(kb * KEYS, KEYS)
                found = lax.dot_general(query, keys[pl.ds(first, KEYS), :], NT, preferred_element_type=F32)
                whole = (first >= start_last) & (first + KEYS <= s)

                def keep(value):
                    scores[slot, :, pl.ds(first, KEYS)] = value
                    top = tops[...]
                    for part in range(KEYS // 128):
                        top = jnp.maximum(top, value[:, part * 128 : (part + 1) * 128])
                    tops[...] = top

                @pl.when(whole)
                def _():
                    keep(found)

                @pl.when(jnp.logical_not(whole))
                def _():
                    spot = first + spots
                    keep(jnp.where((spot >= row_start) & (spot <= s + place), found, LOW))

                return 0

            lax.fori_loop(low, high, step, 0)
            return jnp.max(tops[...], axis=1, keepdims=True) * factor

        def summed(h, slot, top):
            totals[...] = jnp.zeros_like(totals)

            def step(kb, _):
                first = pl.multiple_of(kb * KEYS, KEYS)
                weights = jnp.exp2(scores[slot, :, pl.ds(first, KEYS)] * factor - top).astype(BF16)
                totals[...] += jnp.dot(weights, values[pl.ds(first, KEYS), :], preferred_element_type=F32)
                return 0

            lax.fori_loop(low, high, step, 0)
            out_ref[here, pl.ds(pl.multiple_of(h * DH, DH), DH)] = (totals[:, :DH] / totals[:, DH:]).astype(BF16)

        def one(h, _):
            top = scored(h, 0)
            summed(h, 0, top)
            return 0

        lax.fori_loop(0, heads, one, 0)


def local(doc_lengths, lin_q, lin_k, lin_v, log_decay, lin_gain, soft_q, soft_k, soft_v):
    tokens = lin_q.shape[0]
    heads = lin_gain.shape[0] // DH
    count = lax.axis_size("ctx")
    bits = count.bit_length() - 1
    blocks = tokens // BLK

    head_place = lax.axis_index("head")
    own_keys, own_values = soft_k, soft_v
    for bit in range((lax.axis_size("head") // KVH).bit_length() - 1):
        far_keys, far_values = swapped((own_keys, own_values), "head", bit)
        upper = head_place // (1 << bit) % 2 == 1

        def beside(own, far):
            return jnp.where(upper, jnp.concatenate([far, own], axis=1), jnp.concatenate([own, far], axis=1))

        own_keys, own_values = beside(own_keys, far_keys), beside(own_values, far_values)
    pieces = [jnp.concatenate([own_keys, own_values], axis=1)]
    for bit in range(bits):
        pieces = pieces + [swapped(piece, "ctx", bit) for piece in pieces]

    msg_rows = heads * DH + -(-2 * heads // 16) * 16
    msg = jax.ShapeDtypeStruct((msg_rows, DH), BF16)
    total, first = pl.pallas_call(
        states_kernel,
        out_shape=(msg, jax.ShapeDtypeStruct((max(blocks - 1, 1), heads * DH, DH), BF16)),
        in_specs=[SMEM] + [pl.BlockSpec(memory_space=pltpu.VMEM)] * 3,
        out_specs=(pl.BlockSpec(memory_space=pltpu.VMEM),) * 2,
        name="states",
    )(doc_lengths, lin_k, lin_v, log_decay)

    inside = pl.pallas_call(
        inside_kernel,
        out_shape=jax.ShapeDtypeStruct(lin_q.shape, BF16),
        in_specs=[SMEM] + [pl.BlockSpec(memory_space=pltpu.VMEM)] * 4,
        out_specs=pl.BlockSpec(memory_space=pltpu.VMEM),
        name="inside",
    )(doc_lengths, lin_q, lin_k, lin_v, log_decay)

    prefix = None
    for bit in range(bits - 1):
        far = swapped(total, "ctx", bit)
        if prefix is None:
            def body(t, f, nt, np_, bit=bit):
                combine_kernel(heads, bit, t, None, f, nt, np_)
            operands = (total, far)
        else:
            body = functools.partial(combine_kernel, heads, bit)
            operands = (total, prefix, far)
        total, prefix = pl.pallas_call(
            body,
            out_shape=(msg, msg),
            in_specs=[pl.BlockSpec(memory_space=pltpu.VMEM)] * len(operands),
            out_specs=(pl.BlockSpec(memory_space=pltpu.VMEM),) * 2,
            name="combine",
        )(*operands)
    far = swapped(total, "ctx", bits - 1)

    soft_out = pl.pallas_call(
        functools.partial(softmax_kernel, count),
        out_shape=jax.ShapeDtypeStruct(soft_q.shape, BF16),
        in_specs=[SMEM, pl.BlockSpec(memory_space=pltpu.VMEM)] + [ANY] * count,
        out_specs=pl.BlockSpec(memory_space=pltpu.VMEM),
        scratch_shapes=[
            pltpu.VMEM((count * tokens, DH), BF16),
            pltpu.VMEM((count * tokens, 2 * DH), BF16),
            pltpu.VMEM((1, BLK, count * tokens), F32),
            pltpu.VMEM((BLK, 128), F32),
            pltpu.VMEM((BLK, 2 * DH), F32),
            pltpu.SemaphoreType.DMA((2, count)),
        ],
        compiler_params=pltpu.CompilerParams(vmem_limit_bytes=32 * 1024 * 1024),
        name="softmax",
    )(doc_lengths, soft_q, *pieces)

    lin_out = pl.pallas_call(
        functools.partial(across_kernel, bits - 1),
        out_shape=jax.ShapeDtypeStruct(lin_q.shape, BF16),
        in_specs=[SMEM] + [pl.BlockSpec(memory_space=pltpu.VMEM)] * 7,
        out_specs=pl.BlockSpec(memory_space=pltpu.VMEM),
        name="across",
    )(doc_lengths, lin_q, inside, log_decay, lin_gain.reshape(1, -1), first, prefix, far)
    return (lin_out, soft_out)


def solution(mesh):
    rows = P("ctx", "head")
    placed = (P(), rows, rows, rows, P("head", "ctx"), P("head"), rows, rows, rows)
    return jax.shard_map(
        local, mesh=mesh, in_specs=placed, out_specs=(rows, rows), check_vma=False
    )
```

```python
import functools

import jax
import jax.numpy as jnp
from jax import lax
from jax.experimental import pallas as pl
from jax.experimental.pallas import tpu as pltpu
from jax.sharding import PartitionSpec as P

KVH = 8
DH = 128
BLK = 256
KEYS = 512
ROWS = 256
PLACED = 4.0
LOW = -1e30
LOG2E = 1.4426950408889634
F32 = jnp.float32
BF16 = jnp.bfloat16
NT = (((1,), (1,)), ((), ()))
TN = (((0,), (0,)), ((), ()))
SMEM = pl.BlockSpec(memory_space=pltpu.SMEM)
ANY = pl.BlockSpec(memory_space=pl.ANY)
VMEM = pl.BlockSpec(memory_space=pltpu.VMEM)


def lasting(us):
    return pl.CostEstimate(flops=int(us * 1.1e9), bytes_accessed=0, transcendentals=0)


def swapped(value, axis, bit):
    return lax.ppermute(value, axis, [(i, i ^ 1 << bit) for i in range(lax.axis_size(axis))])


def bounds_of(lengths_ref):
    out, total = [], 0
    for d in range(lengths_ref.shape[0]):
        total = total + lengths_ref[d]
        out.append(total)
    return out


def doc_start(bounds, position):
    start = jnp.zeros_like(position)
    for bound in bounds:
        start = jnp.where(bound <= position, bound, start)
    return start


def log_sums(decay):
    rows = lax.broadcasted_iota(jnp.int32, (BLK, BLK), 0)
    cols = lax.broadcasted_iota(jnp.int32, (BLK, BLK), 1)
    upper = jnp.where(rows <= cols, 1.0, 0.0).astype(BF16)
    terms = []
    for _ in range(3):
        term = decay.astype(BF16).astype(F32)
        terms.append(term)
        decay = decay - term
    stacked = jnp.concatenate(terms, axis=0).astype(BF16)
    found = jnp.dot(stacked, upper, preferred_element_type=F32)
    count = decay.shape[0]
    return found[:count] + found[count : 2 * count] + found[2 * count :]


def states_kernel(lengths_ref, keys_ref, values_ref, decay_ref, msg_ref, first_ref, sums_ref):
    heads = decay_ref.shape[0]
    tokens = keys_ref.shape[0]
    base = lax.axis_index("ctx") * tokens
    bounds = bounds_of(lengths_ref)
    place = lax.broadcasted_iota(jnp.int32, (BLK, 1), 0)
    state = [None] * heads
    through = jnp.ones((heads, 1), F32)
    for b in range(tokens // BLK):
        s = base + b * BLK
        start_last = doc_start(bounds, s + BLK - 1)
        kept = jnp.where(start_last < s, 1.0, 0.0).astype(F32)
        sums = log_sums(decay_ref[:, b * BLK : (b + 1) * BLK])
        sums_ref[:, b * BLK : (b + 1) * BLK] = sums
        closing = sums[:, BLK - 1 : BLK]
        weights = jnp.transpose(jnp.exp(closing - sums), (1, 0))
        weights = jnp.where(s + place >= start_last, weights, 0.0)
        factor = kept * jnp.exp(closing)
        through = through * factor
        for h in range(heads):
            cols = slice(h * DH, (h + 1) * DH)
            keys = keys_ref[b * BLK : (b + 1) * BLK, cols].astype(F32)
            weighted = (keys * weights[:, h : h + 1]).astype(BF16)
            update = lax.dot_general(
                weighted, values_ref[b * BLK : (b + 1) * BLK, cols], TN, preferred_element_type=F32
            )
            if b == 0:
                state[h] = update
            else:
                state[h] = factor[h : h + 1, :] * state[h] + update
            if b < tokens // BLK - 1:
                first_ref[b, h * DH : (h + 1) * DH, :] = update.astype(BF16)
    for h in range(heads):
        msg_ref[h * DH : (h + 1) * DH, :] = state[h].astype(BF16)
    high = through.astype(BF16)
    low = (through - high.astype(F32)).astype(BF16)
    tail = jnp.concatenate([high.astype(F32), low.astype(F32)], axis=0)
    tail = jnp.broadcast_to(tail, (2 * heads, DH))
    extra = msg_ref.shape[0] - heads * DH
    if extra > 2 * heads:
        tail = jnp.concatenate([tail, jnp.zeros((extra - 2 * heads, DH), F32)], axis=0)
    msg_ref[heads * DH :, :] = tail.astype(BF16)


def inside_kernel(lengths_ref, queries_ref, keys_ref, values_ref, sums_ref, out_ref):
    heads = sums_ref.shape[0]
    tokens = keys_ref.shape[0]
    base = lax.axis_index("ctx") * tokens
    bounds = bounds_of(lengths_ref)
    rows = lax.broadcasted_iota(jnp.int32, (BLK, BLK), 0)
    cols = lax.broadcasted_iota(jnp.int32, (BLK, BLK), 1)
    place = lax.broadcasted_iota(jnp.int32, (BLK, 1), 0)
    for b in range(tokens // BLK):
        s = base + b * BLK
        start = doc_start(bounds, s + place) - s
        allowed = (cols <= rows) & (cols >= start)
        sums = sums_ref[:, b * BLK : (b + 1) * BLK]
        down = jnp.transpose(sums, (1, 0))
        here = slice(b * BLK, (b + 1) * BLK)
        for h in range(heads):
            there = slice(h * DH, (h + 1) * DH)
            spread = jnp.where(allowed, down[:, h : h + 1] - sums[h : h + 1, :], LOW)
            scores = lax.dot_general(
                queries_ref[here, there], keys_ref[here, there], NT, preferred_element_type=F32
            )
            scores = (scores * jnp.exp(spread)).astype(BF16)
            out_ref[here, there] = jnp.dot(
                scores, values_ref[here, there], preferred_element_type=F32
            ).astype(BF16)


def through_of(msg_ref, heads, h):
    high = msg_ref[heads * DH + h : heads * DH + h + 1, :].astype(F32)
    low = msg_ref[heads * DH + heads + h : heads * DH + heads + h + 1, :].astype(F32)
    return high + low


def joined(heads, early_ref, late_ref, swap, out_ref):
    def pick(here):
        one, two = early_ref[here, :].astype(F32), late_ref[here, :].astype(F32)
        return jnp.where(swap, two, one), jnp.where(swap, one, two)

    def through(h):
        high = pick(slice(heads * DH + h, heads * DH + h + 1))
        low = pick(slice(heads * DH + heads + h, heads * DH + heads + h + 1))
        return high[0] + low[0], high[1] + low[1]

    tails = []
    for h in range(heads):
        here = slice(h * DH, (h + 1) * DH)
        early, late = pick(here)
        early_through, late_through = through(h)
        out_ref[here, :] = (late_through * early + late).astype(BF16)
        tails.append(late_through * early_through)
    tail = jnp.concatenate(tails, axis=0)
    high = tail.astype(BF16).astype(F32)
    pieces = [high, tail - high]
    extra = out_ref.shape[0] - heads * DH - 2 * heads
    if extra:
        pieces.append(jnp.zeros((extra, DH), F32))
    out_ref[heads * DH :, :] = jnp.concatenate(pieces, axis=0).astype(BF16)


def upper_half(bit):
    return (lax.axis_index("ctx") // (1 << bit)) % 2 == 1


def total_kernel(heads, bit, total_ref, far_ref, new_total_ref):
    joined(heads, total_ref, far_ref, upper_half(bit), new_total_ref)


def prefix_kernel(heads, bit, prefix_ref, far_ref, new_prefix_ref):
    if bit == 1:
        first = jnp.where(upper_half(0), 1.0, 0.0).astype(F32)
        rows = prefix_ref.shape[0]
        tail = lax.broadcasted_iota(jnp.int32, (rows, DH), 0) - heads * DH
        own = prefix_ref[...].astype(F32) * first
        neutral = jnp.where((tail >= 0) & (tail < heads), 1.0 - first, 0.0)
        prefix_ref = (own + neutral).astype(BF16)

    @pl.when(upper_half(bit))
    def _():
        joined(heads, far_ref, prefix_ref, False, new_prefix_ref)

    @pl.when(jnp.logical_not(upper_half(bit)))
    def _():
        new_prefix_ref[...] = prefix_ref[...]


def across_kernel(bit, lengths_ref, queries_ref, inside_ref, sums_ref, gain_ref, first_ref, prefix_ref, far_ref, out_ref):
    heads = sums_ref.shape[0]
    tokens = queries_ref.shape[0]
    place_ctx = lax.axis_index("ctx")
    base = place_ctx * tokens
    upper = jnp.where(upper_half(bit), 1.0, 0.0).astype(F32)
    valid = jnp.where(upper_half(0), 1.0, 0.0).astype(F32) if bit == 1 else 1.0
    bounds = bounds_of(lengths_ref)
    place = lax.broadcasted_iota(jnp.int32, (BLK, 1), 0)
    state = []
    for h in range(heads):
        here = slice(h * DH, (h + 1) * DH)
        through = upper * (valid * through_of(prefix_ref, heads, h) + (1.0 - valid))
        state.append(valid * prefix_ref[here, :].astype(F32) + through * far_ref[here, :].astype(F32))
    for b in range(tokens // BLK):
        s = base + b * BLK
        here = slice(b * BLK, (b + 1) * BLK)
        start_last = doc_start(bounds, s + BLK - 1)
        kept = jnp.where(start_last < s, 1.0, 0.0).astype(F32)
        sums = sums_ref[:, here]
        factor = kept * jnp.exp(sums[:, BLK - 1 : BLK])
        entering = jnp.exp(jnp.transpose(sums, (1, 0)))
        entering = jnp.where(doc_start(bounds, s + place) < s, entering, 0.0)
        for h in range(heads):
            there = slice(h * DH, (h + 1) * DH)
            across = jnp.dot(queries_ref[here, there], state[h].astype(BF16), preferred_element_type=F32)
            raw = inside_ref[here, there].astype(F32) + across * entering[:, h : h + 1]
            scale = lax.rsqrt(jnp.mean(raw * raw, axis=1, keepdims=True) + 1e-06)
            out_ref[here, there] = (raw * scale * gain_ref[:, there]).astype(BF16)
            if b < tokens // BLK - 1:
                state[h] = factor[h : h + 1, :] * state[h] + first_ref[b, there, :].astype(F32)


def softmax_kernel(count, lengths_ref, queries_ref, *refs):
    pieces = refs[:count]
    out_ref, keys, values, scores, tops, totals, sems = refs[count:]
    tokens = queries_ref.shape[0]
    heads = queries_ref.shape[1] // DH
    place_ctx = lax.axis_index("ctx")
    base = place_ctx * tokens
    copies = []
    for m in range(count):
        origin = jnp.int32(0)
        bit = 1
        while bit < count:
            mine = (place_ctx // bit) % 2
            origin = origin + bit * (1 - mine if m & bit else mine)
            bit *= 2
        at = pl.ds(pl.multiple_of(KEYS + origin * tokens, 128), tokens)
        copies.append(pltpu.make_async_copy(pieces[m].at[:, :DH], keys.at[at, :], sems.at[0, m]))
        copies.append(pltpu.make_async_copy(pieces[m].at[:, DH:], values.at[at, :DH], sems.at[1, m]))
    for copy in copies:
        copy.start()
    keys[:KEYS, :] = jnp.zeros((KEYS, DH), BF16)
    values[:KEYS, :DH] = jnp.zeros((KEYS, DH), BF16)
    values[:, DH:] = jnp.ones((values.shape[0], DH), BF16)
    for copy in copies:
        copy.wait()
    bounds = bounds_of(lengths_ref)
    place = lax.broadcasted_iota(jnp.int32, (ROWS, 1), 0)
    spots = lax.broadcasted_iota(jnp.int32, (ROWS, KEYS), 1)
    factor = LOG2E * DH**-0.5
    parts = KEYS // 128

    def row_block(block, _):
        r0 = pl.multiple_of(block * ROWS, ROWS)
        s = base + r0
        row_start = doc_start(bounds, s + place)
        start_half = doc_start(bounds, s + ROWS // 2)
        start_last = doc_start(bounds, s + ROWS - 1)
        steps = (s + ROWS - doc_start(bounds, s) + KEYS - 1) // KEYS

        def first_of(i):
            return s + ROWS - KEYS * (i + 1)

        def at(i):
            return pl.ds(pl.multiple_of(KEYS + first_of(i), 128), KEYS)

        def bias_of(i):
            spot = first_of(i) + spots
            return jnp.where((spot >= row_start) & (spot <= s + place), 0.0, LOW)

        def query(h, rows=ROWS):
            return queries_ref[pl.ds(r0, rows), h * DH : (h + 1) * DH]

        def weighted(found, top):
            spread = [found[:, p * 128 : (p + 1) * 128] * factor - top for p in range(parts)]
            return jnp.concatenate([jnp.exp2(x.astype(BF16)) for x in spread], axis=1)

        bias = bias_of(0)
        key, value = keys[at(0), :], values[at(0), :]
        for h in range(heads):
            here = slice(h * ROWS, (h + 1) * ROWS)
            found = lax.dot_general(query(h), key, NT, preferred_element_type=F32) + bias
            scores[here, :] = found
            top = found[:, :128]
            for p in range(1, parts):
                top = jnp.maximum(top, found[:, p * 128 : (p + 1) * 128])
            top = jnp.max(top, axis=1, keepdims=True) * factor - PLACED
            tops[here, :] = jnp.broadcast_to(top, (ROWS, 128))
        for h in range(heads):
            here = slice(h * ROWS, (h + 1) * ROWS)
            totals[here, :] = jnp.dot(
                weighted(scores[here, :], tops[here, :]), value, preferred_element_type=F32
            )

        def further(i, _):
            def add(bias, rows):
                key, value = keys[at(i), :], values[at(i), :]
                for h in range(heads):
                    here = slice(h * ROWS, h * ROWS + rows)
                    found = lax.dot_general(query(h, rows), key, NT, preferred_element_type=F32)
                    if bias is not None:
                        found = found + bias[:rows]
                    totals[here, :] += jnp.dot(
                        weighted(found, tops[here, :]), value, preferred_element_type=F32
                    )

            whole = first_of(i) >= start_last
            half = first_of(i) + KEYS <= start_half

            @pl.when(whole)
            def _():
                add(None, ROWS)

            @pl.when(jnp.logical_not(whole) & jnp.logical_not(half))
            def _():
                add(bias_of(i), ROWS)

            @pl.when(half)
            def _():
                add(bias_of(i), ROWS // 2)

            return 0

        lax.fori_loop(1, steps, further, 0)

        def settled(rows):
            return jnp.max(totals[rows, DH:]) < 2.0**115

        @pl.when(jnp.logical_not(settled(slice(0, heads * ROWS))))
        def _():
            def one(h, _):
                here = pl.ds(pl.multiple_of(h * ROWS, ROWS), ROWS)

                @pl.when(jnp.logical_not(settled(here)))
                def _():
                    lone = queries_ref[pl.ds(r0, ROWS), pl.ds(pl.multiple_of(h * DH, DH), DH)]

                    def found_of(i):
                        found = lax.dot_general(lone, keys[at(i), :], NT, preferred_element_type=F32)
                        return found + bias_of(i)

                    def highest(i, top):
                        return jnp.maximum(top, jnp.max(found_of(i), axis=1, keepdims=True))

                    top = lax.fori_loop(0, steps, highest, jnp.full((ROWS, 1), LOW, F32))
                    totals[here, :] = jnp.zeros((ROWS, 2 * DH), F32)

                    def add(i, _):
                        weights = jnp.exp2((found_of(i) - top) * factor).astype(BF16)
                        totals[here, :] += jnp.dot(weights, values[at(i), :], preferred_element_type=F32)
                        return 0

                    lax.fori_loop(0, steps, add, 0)

                return 0

            lax.fori_loop(0, heads, one, 0)

        for h in range(heads):
            here = slice(h * ROWS, (h + 1) * ROWS)
            out_ref[pl.ds(r0, ROWS), h * DH : (h + 1) * DH] = (
                totals[here, :DH] / totals[here, DH:]
            ).astype(BF16)
        return 0

    lax.fori_loop(0, tokens // ROWS, row_block, 0)


def local(doc_lengths, lin_q, lin_k, lin_v, log_decay, lin_gain, soft_q, soft_k, soft_v):
    tokens = lin_q.shape[0]
    heads = lin_gain.shape[0] // DH
    count = lax.axis_size("ctx")
    bits = count.bit_length() - 1
    blocks = tokens // BLK

    head_place = lax.axis_index("head")
    own_keys, own_values = soft_k, soft_v
    for bit in range((lax.axis_size("head") // KVH).bit_length() - 1):
        far_keys, far_values = swapped((own_keys, own_values), "head", bit)
        upper = head_place // (1 << bit) % 2 == 1

        def beside(own, far):
            return jnp.where(upper, jnp.concatenate([far, own], axis=1), jnp.concatenate([own, far], axis=1))

        own_keys, own_values = beside(own_keys, far_keys), beside(own_values, far_values)
    pieces = [jnp.concatenate([own_keys, own_values], axis=1)]
    for bit in range(bits):
        pieces = pieces + [swapped(piece, "ctx", bit) for piece in pieces]

    msg_rows = heads * DH + -(-2 * heads // 16) * 16
    msg = jax.ShapeDtypeStruct((msg_rows, DH), BF16)
    total, first, sums = pl.pallas_call(
        states_kernel,
        out_shape=(
            msg,
            jax.ShapeDtypeStruct((max(blocks - 1, 1), heads * DH, DH), BF16),
            jax.ShapeDtypeStruct(log_decay.shape, F32),
        ),
        in_specs=[SMEM] + [VMEM] * 3,
        out_specs=(VMEM,) * 3,
        cost_estimate=lasting(2.5),
        name="states",
    )(doc_lengths, lin_k, lin_v, log_decay)

    inside = pl.pallas_call(
        inside_kernel,
        out_shape=jax.ShapeDtypeStruct(lin_q.shape, BF16),
        in_specs=[SMEM] + [VMEM] * 4,
        out_specs=VMEM,
        cost_estimate=lasting(4),
        name="inside",
    )(doc_lengths, lin_q, lin_k, lin_v, sums)

    prefix = None
    for bit in range(bits - 1):
        far = swapped(total, "ctx", bit)
        if bit == 0:
            prefix = far
        else:
            prefix = pl.pallas_call(
                functools.partial(prefix_kernel, heads, bit),
                out_shape=msg,
                in_specs=[VMEM] * 2,
                out_specs=VMEM,
                name="prefix",
            )(prefix, far)
        total = pl.pallas_call(
            functools.partial(total_kernel, heads, bit),
            out_shape=msg,
            in_specs=[VMEM] * 2,
            out_specs=VMEM,
            cost_estimate=lasting(1),
            name="total",
        )(total, far)
    far = swapped(total, "ctx", bits - 1)

    soft_out = pl.pallas_call(
        functools.partial(softmax_kernel, count),
        out_shape=jax.ShapeDtypeStruct(soft_q.shape, BF16),
        in_specs=[SMEM, VMEM] + [ANY] * count,
        out_specs=VMEM,
        scratch_shapes=[
            pltpu.VMEM((KEYS + count * tokens, DH), BF16),
            pltpu.VMEM((KEYS + count * tokens, 2 * DH), BF16),
            pltpu.VMEM((heads * ROWS, KEYS), F32),
            pltpu.VMEM((heads * ROWS, 128), F32),
            pltpu.VMEM((heads * ROWS, 2 * DH), F32),
            pltpu.SemaphoreType.DMA((2, count)),
        ],
        compiler_params=pltpu.CompilerParams(vmem_limit_bytes=32 * 1024 * 1024),
        cost_estimate=lasting(12),
        name="softmax",
    )(doc_lengths, soft_q, *pieces)

    lin_out = pl.pallas_call(
        functools.partial(across_kernel, bits - 1),
        out_shape=jax.ShapeDtypeStruct(lin_q.shape, BF16),
        in_specs=[SMEM] + [VMEM] * 7,
        out_specs=VMEM,
        cost_estimate=lasting(3),
        name="across",
    )(doc_lengths, lin_q, inside, sums, lin_gain.reshape(1, -1), first, prefix, far)
    return (lin_out, soft_out)


def solution(mesh):
    rows = P("ctx", "head")
    placed = (P(), rows, rows, rows, P("head", "ctx"), P("head"), rows, rows, rows)
    return jax.shard_map(
        local, mesh=mesh, in_specs=placed, out_specs=(rows, rows), check_vma=False
    )
```

```python
import functools

import jax
import jax.numpy as jnp
from jax import lax
from jax.experimental import pallas as pl
from jax.experimental.pallas import tpu as pltpu
from jax.sharding import PartitionSpec as P

KVH = 8
DH = 128
BLK = 256
KEYS = 512
ROWS = 256
PLACED = 4.0
LOW = -1e30
LOG2E = 1.4426950408889634
F32 = jnp.float32
BF16 = jnp.bfloat16
NT = (((1,), (1,)), ((), ()))
TN = (((0,), (0,)), ((), ()))
SMEM = pl.BlockSpec(memory_space=pltpu.SMEM)
ANY = pl.BlockSpec(memory_space=pl.ANY)
VMEM = pl.BlockSpec(memory_space=pltpu.VMEM)


def within(mib):
    return pltpu.CompilerParams(vmem_limit_bytes=mib * 1024 * 1024)


def lasting(us):
    return pl.CostEstimate(flops=int(us * 1.1e9), bytes_accessed=0, transcendentals=0)


def swapped(value, axis, bit):
    return lax.ppermute(value, axis, [(i, i ^ 1 << bit) for i in range(lax.axis_size(axis))])


def bounds_of(lengths_ref):
    out, total = [], 0
    for d in range(lengths_ref.shape[0]):
        total = total + lengths_ref[d]
        out.append(total)
    return out


def doc_start(bounds, position):
    start = jnp.zeros_like(position)
    for bound in bounds:
        start = jnp.where(bound <= position, bound, start)
    return start


def log_sums(decay):
    rows = lax.broadcasted_iota(jnp.int32, (BLK, BLK), 0)
    cols = lax.broadcasted_iota(jnp.int32, (BLK, BLK), 1)
    upper = jnp.where(rows <= cols, 1.0, 0.0).astype(BF16)
    found = jnp.dot(split(decay, 3).astype(BF16), upper, preferred_element_type=F32)
    count = decay.shape[0]
    return found[:count] + found[count : 2 * count] + found[2 * count :]


def split(value, count):
    terms = []
    for _ in range(count):
        term = value.astype(BF16).astype(F32)
        terms.append(term)
        value = value - term
    return jnp.concatenate(terms, axis=0)


def over_lanes(rows_form, count):
    heads = rows_form.shape[0]
    stacked = split(rows_form, count)
    extra = -stacked.shape[0] % 16
    if extra:
        stacked = jnp.concatenate([stacked, jnp.zeros((extra, stacked.shape[1]), F32)], axis=0)
    depth = stacked.shape[0]
    row = lax.broadcasted_iota(jnp.int32, (depth, heads * DH), 0)
    col = lax.broadcasted_iota(jnp.int32, (depth, heads * DH), 1)
    picks = jnp.where((row % heads == col // DH) & (row < count * heads), 1.0, 0.0).astype(BF16)
    return lax.dot_general(stacked.astype(BF16), picks, TN, preferred_element_type=F32)


def states_kernel(lengths_ref, keys_ref, values_ref, decay_ref, msg_ref, first_ref, sums_ref):
    heads = decay_ref.shape[0]
    tokens = keys_ref.shape[0]
    base = lax.axis_index("ctx") * tokens
    bounds = bounds_of(lengths_ref)
    place = lax.broadcasted_iota(jnp.int32, (1, BLK), 1)
    state = [None] * heads
    through = jnp.ones((heads, 1), F32)
    for b in range(tokens // BLK):
        s = base + b * BLK
        start_last = doc_start(bounds, s + BLK - 1)
        kept = jnp.where(start_last < s, 1.0, 0.0).astype(F32)
        sums = log_sums(decay_ref[:, b * BLK : (b + 1) * BLK])
        sums_ref[:, b * BLK : (b + 1) * BLK] = sums
        closing = sums[:, BLK - 1 : BLK]
        weights = jnp.where(s + place >= start_last, jnp.exp(closing - sums), 0.0)
        weights = over_lanes(weights, 2)
        factor = kept * jnp.exp(closing)
        through = through * factor
        for h in range(heads):
            cols = slice(h * DH, (h + 1) * DH)
            keys = keys_ref[b * BLK : (b + 1) * BLK, cols].astype(F32)
            weighted = (keys * weights[:, cols]).astype(BF16)
            update = lax.dot_general(
                weighted, values_ref[b * BLK : (b + 1) * BLK, cols], TN, preferred_element_type=F32
            )
            if b == 0:
                state[h] = update
            else:
                state[h] = factor[h : h + 1, :] * state[h] + update
            if b < tokens // BLK - 1:
                first_ref[b, h * DH : (h + 1) * DH, :] = update.astype(BF16)
    for h in range(heads):
        msg_ref[h * DH : (h + 1) * DH, :] = state[h].astype(BF16)
    tail = jnp.broadcast_to(split(through, 2), (2 * heads, DH))
    extra = msg_ref.shape[0] - heads * DH - 2 * heads
    if extra:
        tail = jnp.concatenate([tail, jnp.zeros((extra, DH), F32)], axis=0)
    msg_ref[heads * DH :, :] = tail.astype(BF16)


def inside_kernel(lengths_ref, queries_ref, keys_ref, values_ref, sums_ref, out_ref):
    heads = sums_ref.shape[0]
    tokens = keys_ref.shape[0]
    base = lax.axis_index("ctx") * tokens
    bounds = bounds_of(lengths_ref)
    rows = lax.broadcasted_iota(jnp.int32, (BLK, BLK), 0)
    cols = lax.broadcasted_iota(jnp.int32, (BLK, BLK), 1)
    place = lax.broadcasted_iota(jnp.int32, (BLK, 1), 0)
    for b in range(tokens // BLK):
        s = base + b * BLK
        start = doc_start(bounds, s + place) - s
        bias = jnp.where((cols <= rows) & (cols >= start), 0.0, LOW)
        here = slice(b * BLK, (b + 1) * BLK)
        sums = sums_ref[:, here] * LOG2E
        down = over_lanes(sums, 3)
        for h in range(heads):
            there = slice(h * DH, (h + 1) * DH)
            upright = jnp.concatenate([down[:, there]] * (BLK // DH), axis=1)
            spread = upright - sums[h : h + 1, :] + bias
            scores = lax.dot_general(
                queries_ref[here, there], keys_ref[here, there], NT, preferred_element_type=F32
            )
            scores = (scores * jnp.exp2(spread)).astype(BF16)
            out_ref[here, there] = jnp.dot(
                scores, values_ref[here, there], preferred_element_type=F32
            ).astype(BF16)


def through_of(msg_ref, heads, h):
    high = msg_ref[heads * DH + h : heads * DH + h + 1, :].astype(F32)
    low = msg_ref[heads * DH + heads + h : heads * DH + heads + h + 1, :].astype(F32)
    return high + low


def joined(heads, early_ref, late_ref, swap, out_ref):
    def pick(here):
        one, two = early_ref[here, :].astype(F32), late_ref[here, :].astype(F32)
        return jnp.where(swap, two, one), jnp.where(swap, one, two)

    def through(h):
        high = pick(slice(heads * DH + h, heads * DH + h + 1))
        low = pick(slice(heads * DH + heads + h, heads * DH + heads + h + 1))
        return high[0] + low[0], high[1] + low[1]

    tails = []
    for h in range(heads):
        here = slice(h * DH, (h + 1) * DH)
        early, late = pick(here)
        early_through, late_through = through(h)
        out_ref[here, :] = (late_through * early + late).astype(BF16)
        tails.append(late_through * early_through)
    tail = jnp.concatenate(tails, axis=0)
    high = tail.astype(BF16).astype(F32)
    pieces = [high, tail - high]
    extra = out_ref.shape[0] - heads * DH - 2 * heads
    if extra:
        pieces.append(jnp.zeros((extra, DH), F32))
    out_ref[heads * DH :, :] = jnp.concatenate(pieces, axis=0).astype(BF16)


def upper_half(bit):
    return (lax.axis_index("ctx") // (1 << bit)) % 2 == 1


def total_kernel(heads, bit, total_ref, far_ref, new_total_ref):
    joined(heads, total_ref, far_ref, upper_half(bit), new_total_ref)


def prefix_kernel(heads, bit, prefix_ref, far_ref, new_prefix_ref):
    if bit == 1:
        first = jnp.where(upper_half(0), 1.0, 0.0).astype(F32)
        rows = prefix_ref.shape[0]
        tail = lax.broadcasted_iota(jnp.int32, (rows, DH), 0) - heads * DH
        own = prefix_ref[...].astype(F32) * first
        neutral = jnp.where((tail >= 0) & (tail < heads), 1.0 - first, 0.0)
        prefix_ref = (own + neutral).astype(BF16)

    @pl.when(upper_half(bit))
    def _():
        joined(heads, far_ref, prefix_ref, False, new_prefix_ref)

    @pl.when(jnp.logical_not(upper_half(bit)))
    def _():
        new_prefix_ref[...] = prefix_ref[...]


def across_kernel(bit, lengths_ref, queries_ref, inside_ref, sums_ref, gain_ref, first_ref, prefix_ref, far_ref, out_ref):
    heads = sums_ref.shape[0]
    tokens = queries_ref.shape[0]
    place_ctx = lax.axis_index("ctx")
    base = place_ctx * tokens
    upper = jnp.where(upper_half(bit), 1.0, 0.0).astype(F32)
    valid = jnp.where(upper_half(0), 1.0, 0.0).astype(F32) if bit == 1 else 1.0
    bounds = bounds_of(lengths_ref)
    place = lax.broadcasted_iota(jnp.int32, (1, BLK), 1)
    state = []
    for h in range(heads):
        here = slice(h * DH, (h + 1) * DH)
        through = upper * (valid * through_of(prefix_ref, heads, h) + (1.0 - valid))
        state.append(valid * prefix_ref[here, :].astype(F32) + through * far_ref[here, :].astype(F32))
    ones = jnp.ones((DH, DH), BF16)
    for b in range(tokens // BLK):
        s = base + b * BLK
        here = slice(b * BLK, (b + 1) * BLK)
        start_last = doc_start(bounds, s + BLK - 1)
        kept = jnp.where(start_last < s, 1.0, 0.0).astype(F32)
        sums = sums_ref[:, here]
        factor = kept * jnp.exp(sums[:, BLK - 1 : BLK])
        entering = jnp.where(doc_start(bounds, s + place) < s, jnp.exp(sums), 0.0)
        entering = over_lanes(entering, 2)
        for h in range(heads):
            there = slice(h * DH, (h + 1) * DH)
            across = jnp.dot(queries_ref[here, there], state[h].astype(BF16), preferred_element_type=F32)
            raw = inside_ref[here, there].astype(F32) + across * entering[:, there]
            square = jnp.dot((raw * raw).astype(BF16), ones, preferred_element_type=F32)
            scale = lax.rsqrt(square * (1.0 / DH) + 1e-06)
            out_ref[here, there] = (raw * scale * gain_ref[:, there]).astype(BF16)
            if b < tokens // BLK - 1:
                state[h] = factor[h : h + 1, :] * state[h] + first_ref[b, there, :].astype(F32)


def softmax_kernel(count, lengths_ref, queries_ref, *refs):
    pieces = refs[:count]
    out_ref, keys, values, scores, tops, totals, sems = refs[count:]
    tokens = queries_ref.shape[0]
    heads = queries_ref.shape[1] // DH
    place_ctx = lax.axis_index("ctx")
    base = place_ctx * tokens
    copies = []
    for m in range(count):
        origin = jnp.int32(0)
        bit = 1
        while bit < count:
            mine = (place_ctx // bit) % 2
            origin = origin + bit * (1 - mine if m & bit else mine)
            bit *= 2
        at = pl.ds(pl.multiple_of(KEYS + origin * tokens, 128), tokens)
        copies.append(pltpu.make_async_copy(pieces[m].at[:, :DH], keys.at[at, :], sems.at[0, m]))
        copies.append(pltpu.make_async_copy(pieces[m].at[:, DH:], values.at[at, :DH], sems.at[1, m]))
    for copy in copies:
        copy.start()
    keys[:KEYS, :] = jnp.zeros((KEYS, DH), BF16)
    values[:KEYS, :DH] = jnp.zeros((KEYS, DH), BF16)
    values[:, DH:] = jnp.ones((values.shape[0], DH), BF16)
    for copy in copies:
        copy.wait()
    bounds = bounds_of(lengths_ref)
    place = lax.broadcasted_iota(jnp.int32, (ROWS, 1), 0)
    spots = lax.broadcasted_iota(jnp.int32, (ROWS, KEYS), 1)
    factor = LOG2E * DH**-0.5
    parts = KEYS // 128

    def row_block(block, _):
        r0 = pl.multiple_of(block * ROWS, ROWS)
        s = base + r0
        row_start = doc_start(bounds, s + place)
        start_half = doc_start(bounds, s + ROWS // 2)
        start_last = doc_start(bounds, s + ROWS - 1)
        steps = (s + ROWS - doc_start(bounds, s) + KEYS - 1) // KEYS

        def first_of(i):
            return s + ROWS - KEYS * (i + 1)

        def at(i):
            return pl.ds(pl.multiple_of(KEYS + first_of(i), 128), KEYS)

        def bias_of(i):
            spot = first_of(i) + spots
            return jnp.where((spot >= row_start) & (spot <= s + place), 0.0, LOW)

        def query(h, rows=ROWS):
            return queries_ref[pl.ds(r0, rows), h * DH : (h + 1) * DH]

        def weighted(found, top):
            spread = [found[:, p * 128 : (p + 1) * 128] * factor - top for p in range(parts)]
            return jnp.concatenate([jnp.exp2(x.astype(BF16)) for x in spread], axis=1)

        bias = bias_of(0)
        key, value = keys[at(0), :], values[at(0), :]
        for h in range(heads):
            here = slice(h * ROWS, (h + 1) * ROWS)
            found = lax.dot_general(query(h), key, NT, preferred_element_type=F32) + bias
            scores[here, :] = found
            top = found[:, :128]
            for p in range(1, parts):
                top = jnp.maximum(top, found[:, p * 128 : (p + 1) * 128])
            top = jnp.max(top, axis=1, keepdims=True) * factor - PLACED
            tops[here, :] = jnp.broadcast_to(top, (ROWS, 128))
        for h in range(heads):
            here = slice(h * ROWS, (h + 1) * ROWS)
            totals[here, :] = jnp.dot(
                weighted(scores[here, :], tops[here, :]), value, preferred_element_type=F32
            )

        def further(i, _):
            def add(bias, rows):
                key, value = keys[at(i), :], values[at(i), :]
                for h in range(heads):
                    here = slice(h * ROWS, h * ROWS + rows)
                    found = lax.dot_general(query(h, rows), key, NT, preferred_element_type=F32)
                    if bias is not None:
                        found = found + bias[:rows]
                    totals[here, :] += jnp.dot(
                        weighted(found, tops[here, :]), value, preferred_element_type=F32
                    )

            whole = first_of(i) >= start_last
            half = first_of(i) + KEYS <= start_half

            @pl.when(whole)
            def _():
                add(None, ROWS)

            @pl.when(jnp.logical_not(whole) & jnp.logical_not(half))
            def _():
                add(bias_of(i), ROWS)

            @pl.when(half)
            def _():
                add(bias_of(i), ROWS // 2)

            return 0

        lax.fori_loop(1, steps, further, 0)

        def settled(rows):
            return jnp.max(totals[rows, DH:]) < 2.0**115

        @pl.when(jnp.logical_not(settled(slice(0, heads * ROWS))))
        def _():
            def one(h, _):
                here = pl.ds(pl.multiple_of(h * ROWS, ROWS), ROWS)

                @pl.when(jnp.logical_not(settled(here)))
                def _():
                    lone = queries_ref[pl.ds(r0, ROWS), pl.ds(pl.multiple_of(h * DH, DH), DH)]

                    def found_of(i):
                        found = lax.dot_general(lone, keys[at(i), :], NT, preferred_element_type=F32)
                        return found + bias_of(i)

                    def highest(i, top):
                        return jnp.maximum(top, jnp.max(found_of(i), axis=1, keepdims=True))

                    top = lax.fori_loop(0, steps, highest, jnp.full((ROWS, 1), LOW, F32))
                    totals[here, :] = jnp.zeros((ROWS, 2 * DH), F32)

                    def add(i, _):
                        weights = jnp.exp2((found_of(i) - top) * factor).astype(BF16)
                        totals[here, :] += jnp.dot(weights, values[at(i), :], preferred_element_type=F32)
                        return 0

                    lax.fori_loop(0, steps, add, 0)

                return 0

            lax.fori_loop(0, heads, one, 0)

        for h in range(heads):
            here = slice(h * ROWS, (h + 1) * ROWS)
            out_ref[pl.ds(r0, ROWS), h * DH : (h + 1) * DH] = (
                totals[here, :DH] / totals[here, DH:]
            ).astype(BF16)
        return 0

    lax.fori_loop(0, tokens // ROWS, row_block, 0)


def local(doc_lengths, lin_q, lin_k, lin_v, log_decay, lin_gain, soft_q, soft_k, soft_v):
    tokens = lin_q.shape[0]
    heads = lin_gain.shape[0] // DH
    count = lax.axis_size("ctx")
    bits = count.bit_length() - 1
    blocks = tokens // BLK

    head_place = lax.axis_index("head")
    own_keys, own_values = soft_k, soft_v
    for bit in range((lax.axis_size("head") // KVH).bit_length() - 1):
        far_keys, far_values = swapped((own_keys, own_values), "head", bit)
        upper = head_place // (1 << bit) % 2 == 1

        def beside(own, far):
            return jnp.where(upper, jnp.concatenate([far, own], axis=1), jnp.concatenate([own, far], axis=1))

        own_keys, own_values = beside(own_keys, far_keys), beside(own_values, far_values)
    pieces = [jnp.concatenate([own_keys, own_values], axis=1)]
    for bit in range(bits):
        pieces = pieces + [swapped(piece, "ctx", bit) for piece in pieces]

    msg_rows = heads * DH + -(-2 * heads // 16) * 16
    msg = jax.ShapeDtypeStruct((msg_rows, DH), BF16)
    total, first, sums = pl.pallas_call(
        states_kernel,
        out_shape=(
            msg,
            jax.ShapeDtypeStruct((max(blocks - 1, 1), heads * DH, DH), BF16),
            jax.ShapeDtypeStruct(log_decay.shape, F32),
        ),
        in_specs=[SMEM] + [VMEM] * 3,
        out_specs=(VMEM,) * 3,
        cost_estimate=lasting(2.5),
        compiler_params=within(12),
        name="states",
    )(doc_lengths, lin_k, lin_v, log_decay)

    inside = pl.pallas_call(
        inside_kernel,
        out_shape=jax.ShapeDtypeStruct(lin_q.shape, BF16),
        in_specs=[SMEM] + [VMEM] * 4,
        out_specs=VMEM,
        cost_estimate=lasting(4),
        compiler_params=within(12),
        name="inside",
    )(doc_lengths, lin_q, lin_k, lin_v, sums)

    prefix = None
    for bit in range(bits - 1):
        far = swapped(total, "ctx", bit)
        if bit == 0:
            prefix = far
        else:
            prefix = pl.pallas_call(
                functools.partial(prefix_kernel, heads, bit),
                out_shape=msg,
                in_specs=[VMEM] * 2,
                out_specs=VMEM,
                compiler_params=within(8),
        name="prefix",
            )(prefix, far)
        total = pl.pallas_call(
            functools.partial(total_kernel, heads, bit),
            out_shape=msg,
            in_specs=[VMEM] * 2,
            out_specs=VMEM,
            cost_estimate=lasting(1),
            compiler_params=within(8),
        name="total",
        )(total, far)
    far = swapped(total, "ctx", bits - 1)

    soft_out = pl.pallas_call(
        functools.partial(softmax_kernel, count),
        out_shape=jax.ShapeDtypeStruct(soft_q.shape, BF16),
        in_specs=[SMEM, VMEM] + [ANY] * count,
        out_specs=VMEM,
        scratch_shapes=[
            pltpu.VMEM((KEYS + count * tokens, DH), BF16),
            pltpu.VMEM((KEYS + count * tokens, 2 * DH), BF16),
            pltpu.VMEM((heads * ROWS, KEYS), F32),
            pltpu.VMEM((heads * ROWS, 128), F32),
            pltpu.VMEM((heads * ROWS, 2 * DH), F32),
            pltpu.SemaphoreType.DMA((2, count)),
        ],
        compiler_params=within(24),
        cost_estimate=lasting(12),
        name="softmax",
    )(doc_lengths, soft_q, *pieces)

    lin_out = pl.pallas_call(
        functools.partial(across_kernel, bits - 1),
        out_shape=jax.ShapeDtypeStruct(lin_q.shape, BF16),
        in_specs=[SMEM] + [VMEM] * 7,
        out_specs=VMEM,
        cost_estimate=lasting(3),
        compiler_params=within(12),
        name="across",
    )(doc_lengths, lin_q, inside, sums, lin_gain.reshape(1, -1), first, prefix, far)
    return (lin_out, soft_out)


def solution(mesh):
    rows = P("ctx", "head")
    placed = (P(), rows, rows, rows, P("head", "ctx"), P("head"), rows, rows, rows)
    return jax.shard_map(
        local, mesh=mesh, in_specs=placed, out_specs=(rows, rows), check_vma=False
    )
```

```python
import functools

import jax
import jax.numpy as jnp
from jax import lax
from jax.experimental import pallas as pl
from jax.experimental.pallas import tpu as pltpu
from jax.sharding import PartitionSpec as P

KVH = 8
DH = 128
BLK = 256
ROWS = 256
PLACED = 90.0
LOW = -1e30
LOG2E = 1.4426950408889634
FACTOR = LOG2E * DH**-0.5
F32 = jnp.float32
BF16 = jnp.bfloat16
NT = (((1,), (1,)), ((), ()))
TN = (((0,), (0,)), ((), ()))
HBM = pl.BlockSpec(memory_space=pltpu.HBM)
VMEM = pl.BlockSpec(memory_space=pltpu.VMEM)


def within(mib):
    return pltpu.CompilerParams(vmem_limit_bytes=mib * 1024 * 1024)


def lasting(us):
    return pl.CostEstimate(flops=int(us * 0.8e9), bytes_accessed=0, transcendentals=0)


def swapped(value, axis, bit):
    return lax.ppermute(value, axis, [(i, i ^ 1 << bit) for i in range(lax.axis_size(axis))])


def bounds_of(lengths_ref):
    out, total = [], 0
    lengths = lengths_ref[...]
    for d in range(lengths.shape[1]):
        total = total + lengths[0, d]
        out.append(total)
    return out


def doc_start(bounds, position):
    start = jnp.zeros_like(position)
    for bound in bounds:
        start = jnp.where(bound <= position, bound, start)
    return start


def log_sums(decay):
    rows = lax.broadcasted_iota(jnp.int32, (BLK, BLK), 0)
    cols = lax.broadcasted_iota(jnp.int32, (BLK, BLK), 1)
    upper = jnp.where(rows <= cols, 1.0, 0.0).astype(BF16)
    found = jnp.dot(split(decay, 3).astype(BF16), upper, preferred_element_type=F32)
    count = decay.shape[0]
    return found[:count] + found[count : 2 * count] + found[2 * count :]


def split(value, count):
    terms = []
    for _ in range(count):
        term = value.astype(BF16).astype(F32)
        terms.append(term)
        value = value - term
    return jnp.concatenate(terms, axis=0)


def over_lanes(rows_form, count):
    heads = rows_form.shape[0]
    stacked = split(rows_form, count)
    extra = -stacked.shape[0] % 16
    if extra:
        stacked = jnp.concatenate([stacked, jnp.zeros((extra, stacked.shape[1]), F32)], axis=0)
    depth = stacked.shape[0]
    row = lax.broadcasted_iota(jnp.int32, (depth, heads * DH), 0)
    col = lax.broadcasted_iota(jnp.int32, (depth, heads * DH), 1)
    picks = jnp.where((row % heads == col // DH) & (row < count * heads), 1.0, 0.0).astype(BF16)
    return lax.dot_general(stacked.astype(BF16), picks, TN, preferred_element_type=F32)


def states_kernel(lengths_ref, keys_hbm, values_hbm, decay_ref, msg_ref, first_ref, sums_ref, keys_ref, values_ref, sems):
    heads = decay_ref.shape[0]
    tokens = keys_ref.shape[0]
    base = lax.axis_index("ctx") * tokens
    bounds = bounds_of(lengths_ref)
    place = lax.broadcasted_iota(jnp.int32, (1, BLK), 1)
    blocks = tokens // BLK
    copies = []
    for b in range(blocks):
        rows = slice(b * BLK, (b + 1) * BLK)
        copies.append(pltpu.make_async_copy(keys_hbm.at[rows, :], keys_ref.at[rows, :], sems.at[0, b]))
        copies.append(pltpu.make_async_copy(values_hbm.at[rows, :], values_ref.at[rows, :], sems.at[1, b]))
    for copy in copies:
        copy.start()
    through = jnp.ones((heads, 1), F32)
    weights, factors = [], []
    for b in range(blocks):
        s = base + b * BLK
        start_last = doc_start(bounds, s + BLK - 1)
        kept = jnp.where(start_last < s, 1.0, 0.0).astype(F32)
        sums = log_sums(decay_ref[:, b * BLK : (b + 1) * BLK])
        sums_ref[:, b * BLK : (b + 1) * BLK] = sums
        closing = sums[:, BLK - 1 : BLK]
        weight = jnp.where(s + place >= start_last, jnp.exp(closing - sums), 0.0)
        weights.append(over_lanes(weight, 2))
        factors.append(kept * jnp.exp(closing))
        through = through * factors[b]
    state = [None] * heads
    for b in range(blocks):
        copies[2 * b].wait()
        copies[2 * b + 1].wait()
        rows = slice(b * BLK, (b + 1) * BLK)
        for h in range(heads):
            cols = slice(h * DH, (h + 1) * DH)
            weighted = (keys_ref[rows, cols].astype(F32) * weights[b][:, cols]).astype(BF16)
            update = lax.dot_general(weighted, values_ref[rows, cols], TN, preferred_element_type=F32)
            state[h] = update if b == 0 else factors[b][h : h + 1, :] * state[h] + update
            if b < blocks - 1:
                first_ref[b, cols, :] = update.astype(BF16)
    for h in range(heads):
        msg_ref[h * DH : (h + 1) * DH, :] = state[h].astype(BF16)
    tail = jnp.broadcast_to(split(through, 2), (2 * heads, DH))
    extra = msg_ref.shape[0] - heads * DH - 2 * heads
    if extra:
        tail = jnp.concatenate([tail, jnp.zeros((extra, DH), F32)], axis=0)
    msg_ref[heads * DH :, :] = tail.astype(BF16)


def inside_kernel(lengths_ref, queries_ref, keys_ref, values_ref, sums_ref, out_ref):
    heads = sums_ref.shape[0]
    tokens = keys_ref.shape[0]
    base = lax.axis_index("ctx") * tokens
    bounds = bounds_of(lengths_ref)
    rows = lax.broadcasted_iota(jnp.int32, (BLK, BLK), 0)
    cols = lax.broadcasted_iota(jnp.int32, (BLK, BLK), 1)
    place = lax.broadcasted_iota(jnp.int32, (BLK, 1), 0)
    for b in range(tokens // BLK):
        s = base + b * BLK
        start = doc_start(bounds, s + place) - s
        bias = jnp.where((cols <= rows) & (cols >= start), 0.0, LOW)
        here = slice(b * BLK, (b + 1) * BLK)
        sums = sums_ref[:, here] * LOG2E
        down = over_lanes(sums, 3)
        for h in range(heads):
            there = slice(h * DH, (h + 1) * DH)
            upright = jnp.concatenate([down[:, there]] * (BLK // DH), axis=1)
            spread = upright - sums[h : h + 1, :] + bias
            scores = lax.dot_general(
                queries_ref[here, there], keys_ref[here, there], NT, preferred_element_type=F32
            )
            scores = (scores * jnp.exp2(spread)).astype(BF16)
            out_ref[here, there] = jnp.dot(
                scores, values_ref[here, there], preferred_element_type=F32
            ).astype(BF16)


def through_of(msg_ref, heads, h):
    high = msg_ref[heads * DH + h : heads * DH + h + 1, :].astype(F32)
    low = msg_ref[heads * DH + heads + h : heads * DH + heads + h + 1, :].astype(F32)
    return high + low


def joined(heads, early_ref, late_ref, swap, out_ref):
    def pick(here):
        one, two = early_ref[here, :].astype(F32), late_ref[here, :].astype(F32)
        return jnp.where(swap, two, one), jnp.where(swap, one, two)

    def through(h):
        high = pick(slice(heads * DH + h, heads * DH + h + 1))
        low = pick(slice(heads * DH + heads + h, heads * DH + heads + h + 1))
        return high[0] + low[0], high[1] + low[1]

    tails = []
    for h in range(heads):
        here = slice(h * DH, (h + 1) * DH)
        early, late = pick(here)
        early_through, late_through = through(h)
        out_ref[here, :] = (late_through * early + late).astype(BF16)
        tails.append(late_through * early_through)
    tail = jnp.concatenate(tails, axis=0)
    high = tail.astype(BF16).astype(F32)
    pieces = [high, tail - high]
    extra = out_ref.shape[0] - heads * DH - 2 * heads
    if extra:
        pieces.append(jnp.zeros((extra, DH), F32))
    out_ref[heads * DH :, :] = jnp.concatenate(pieces, axis=0).astype(BF16)


def upper_half(bit):
    return (lax.axis_index("ctx") // (1 << bit)) % 2 == 1


def total_kernel(heads, bit, total_ref, far_ref, new_total_ref):
    joined(heads, total_ref, far_ref, upper_half(bit), new_total_ref)


def prefix_kernel(heads, bit, prefix_ref, far_ref, new_prefix_ref):
    if bit == 1:
        first = jnp.where(upper_half(0), 1.0, 0.0).astype(F32)
        rows = prefix_ref.shape[0]
        tail = lax.broadcasted_iota(jnp.int32, (rows, DH), 0) - heads * DH
        own = prefix_ref[...].astype(F32) * first
        neutral = jnp.where((tail >= 0) & (tail < heads), 1.0 - first, 0.0)
        prefix_ref = (own + neutral).astype(BF16)

    @pl.when(upper_half(bit))
    def _():
        joined(heads, far_ref, prefix_ref, False, new_prefix_ref)

    @pl.when(jnp.logical_not(upper_half(bit)))
    def _():
        new_prefix_ref[...] = prefix_ref[...]


def across_kernel(
    bit, lengths_ref, queries_ref, inside_ref, sums_ref, gain_ref, first_ref, prefix_ref, far_ref, soft_ref,
    out_hbm, soft_hbm, out_ref, sems,
):
    soft_copy = pltpu.make_async_copy(soft_ref, soft_hbm, sems.at[0])
    soft_copy.start()
    copies = []
    heads = sums_ref.shape[0]
    tokens = queries_ref.shape[0]
    place_ctx = lax.axis_index("ctx")
    base = place_ctx * tokens
    upper = jnp.where(upper_half(bit), 1.0, 0.0).astype(F32)
    valid = jnp.where(upper_half(0), 1.0, 0.0).astype(F32) if bit == 1 else 1.0
    bounds = bounds_of(lengths_ref)
    place = lax.broadcasted_iota(jnp.int32, (1, BLK), 1)
    state = []
    for h in range(heads):
        here = slice(h * DH, (h + 1) * DH)
        through = upper * (valid * through_of(prefix_ref, heads, h) + (1.0 - valid))
        state.append(valid * prefix_ref[here, :].astype(F32) + through * far_ref[here, :].astype(F32))
    ones = jnp.ones((DH, DH), BF16)
    for b in range(tokens // BLK):
        s = base + b * BLK
        here = slice(b * BLK, (b + 1) * BLK)
        start_last = doc_start(bounds, s + BLK - 1)
        kept = jnp.where(start_last < s, 1.0, 0.0).astype(F32)
        sums = sums_ref[:, here]
        factor = kept * jnp.exp(sums[:, BLK - 1 : BLK])
        entering = jnp.where(doc_start(bounds, s + place) < s, jnp.exp(sums), 0.0)
        entering = over_lanes(entering, 2)
        for h in range(heads):
            there = slice(h * DH, (h + 1) * DH)
            across = jnp.dot(queries_ref[here, there], state[h].astype(BF16), preferred_element_type=F32)
            raw = inside_ref[here, there].astype(F32) + across * entering[:, there]
            square = jnp.dot((raw * raw).astype(BF16), ones, preferred_element_type=F32)
            scale = lax.rsqrt(square * (1.0 / DH) + 1e-06)
            out_ref[here, there] = (raw * scale * gain_ref[:, there]).astype(BF16)
            if b < tokens // BLK - 1:
                state[h] = factor[h : h + 1, :] * state[h] + first_ref[b, there, :].astype(F32)
        copies.append(pltpu.make_async_copy(out_ref.at[here, :], out_hbm.at[here, :], sems.at[1 + b]))
        copies[b].start()
    soft_copy.wait()
    for copy in copies:
        copy.wait()


def origin_of(m, count):
    place = lax.axis_index("ctx")
    origin = jnp.int32(0)
    bit = 1
    while bit < count:
        mine = (place // bit) % 2
        origin = origin + bit * (1 - mine if m & bit else mine)
        bit *= 2
    return origin


def bias_of(bounds, first_row, rows, first_key, count):
    row = first_row + lax.broadcasted_iota(jnp.int32, (rows, 1), 0)
    key = first_key + lax.broadcasted_iota(jnp.int32, (rows, count), 1)
    return jnp.where((key >= doc_start(bounds, row)) & (key <= row), 0.0, LOW)


def with_ones(values):
    return jnp.concatenate([values, jnp.ones(values.shape, BF16)], axis=1)


def weighted(found, top):
    spread = [found[:, p : p + 128] * FACTOR - top for p in range(0, found.shape[1], 128)]
    return jnp.concatenate([jnp.exp2(x).astype(BF16) for x in spread], axis=1)


def near_kernel(lengths_ref, queries_ref, own_ref, totals_ref, tops_ref, scores):
    tokens = queries_ref.shape[0]
    heads = queries_ref.shape[1] // DH
    base = lax.axis_index("ctx") * tokens
    bounds = bounds_of(lengths_ref)
    for block in range(tokens // ROWS):
        count = (block + 1) * ROWS
        rows = slice(block * ROWS, (block + 1) * ROWS)
        bias = bias_of(bounds, base + block * ROWS, ROWS, base, count)
        key, value = own_ref[:count, :], with_ones(own_ref[tokens : tokens + count, :])
        for h in range(heads):
            there = slice(h * ROWS, (h + 1) * ROWS)
            at = slice((block * heads + h) * ROWS, (block * heads + h + 1) * ROWS)
            found = lax.dot_general(
                queries_ref[rows, h * DH : (h + 1) * DH], key, NT, preferred_element_type=F32
            )
            found = found + bias
            scores[there, :count] = found
            top = found[:, :128]
            for p in range(128, count, 128):
                top = jnp.maximum(top, found[:, p : p + 128])
            top = jnp.max(top, axis=1, keepdims=True) * FACTOR + PLACED
            tops_ref[at, :] = jnp.broadcast_to(top, (ROWS, 128))
        for h in range(heads):
            there = slice(h * ROWS, (h + 1) * ROWS)
            at = slice((block * heads + h) * ROWS, (block * heads + h + 1) * ROWS)
            totals_ref[at, :] = jnp.dot(
                weighted(scores[there, :count], tops_ref[at, :]), value, preferred_element_type=F32
            )


def add_piece(bounds, base, block, origin, queries_ref, piece_ref, totals_ref, tops_ref):
    tokens = queries_ref.shape[0]
    heads = queries_ref.shape[1] // DH
    s = base + block * ROWS
    first = origin * tokens
    needed = (first < base) & (first + tokens > doc_start(bounds, s))
    whole = first >= doc_start(bounds, s + ROWS - 1)
    half = first + tokens <= doc_start(bounds, s + ROWS // 2)

    def add(bias, rows):
        key, value = piece_ref[:tokens, :], with_ones(piece_ref[tokens:, :])
        for h in range(heads):
            at = pl.ds(pl.multiple_of((block * heads + h) * ROWS, ROWS), rows)
            query = queries_ref[pl.ds(pl.multiple_of(block * ROWS, ROWS), rows), h * DH : (h + 1) * DH]
            found = lax.dot_general(query, key, NT, preferred_element_type=F32)
            if bias is not None:
                found = found + bias
            totals_ref[at, :] += jnp.dot(weighted(found, tops_ref[at, :]), value, preferred_element_type=F32)

    @pl.when(needed & whole)
    def _():
        add(None, ROWS)

    @pl.when(needed & jnp.logical_not(whole) & jnp.logical_not(half))
    def _():
        add(bias_of(bounds, s, ROWS, first, tokens), ROWS)

    @pl.when(needed & half)
    def _():
        add(bias_of(bounds, s, ROWS // 2, first, tokens), ROWS // 2)


def middle_kernel(count, which, lengths_ref, queries_ref, tops_ref, totals_in, *refs):
    pieces, totals_ref = refs[:-1], refs[-1]
    tokens = queries_ref.shape[0]
    base = lax.axis_index("ctx") * tokens
    bounds = bounds_of(lengths_ref)

    def row_block(block, _):
        for m, piece_ref in zip(which, pieces):
            add_piece(bounds, base, block, origin_of(m, count), queries_ref, piece_ref, totals_ref, tops_ref)
        return 0

    lax.fori_loop(0, tokens // ROWS, row_block, 0)


def last_kernel(count, which, lengths_ref, queries_ref, tops_ref, totals_in, *refs):
    pieces, out_ref, totals_ref = refs[:count], refs[count], refs[count + 1]
    tokens = queries_ref.shape[0]
    heads = queries_ref.shape[1] // DH
    base = lax.axis_index("ctx") * tokens
    bounds = bounds_of(lengths_ref)

    def row_block(block, _):
        for m in which:
            add_piece(bounds, base, block, origin_of(m, count), queries_ref, pieces[m], totals_ref, tops_ref)
        return 0

    lax.fori_loop(0, tokens // ROWS, row_block, 0)

    def divided(block, h):
        at = pl.ds(pl.multiple_of((block * heads + h) * ROWS, ROWS), ROWS)
        total = totals_ref[at, DH:]
        return (totals_ref[at, :DH] * pl.reciprocal(total, approx=True)).astype(BF16), total

    highest = jnp.zeros((ROWS, DH), F32)
    for block in range(tokens // ROWS):
        for h in range(heads):
            found, total = divided(block, h)
            out_ref[block * ROWS : (block + 1) * ROWS, h * DH : (h + 1) * DH] = found
            highest = jnp.maximum(highest, total)

    def again(block, h, at):
        s = base + block * ROWS
        rows = pl.ds(pl.multiple_of(block * ROWS, ROWS), ROWS)
        cols = pl.ds(pl.multiple_of(h * DH, DH), DH)
        query = queries_ref[rows, cols]

        def found_of(m):
            found = lax.dot_general(query, pieces[m][:tokens, :], NT, preferred_element_type=F32)
            return found + bias_of(bounds, s, ROWS, origin_of(m, count) * tokens, tokens)

        top = jnp.full((ROWS, 1), LOW, F32)
        for m in range(count):
            top = jnp.maximum(top, jnp.max(found_of(m), axis=1, keepdims=True))
        totals_ref[at, :] = jnp.zeros((ROWS, 2 * DH), F32)
        for m in range(count):
            weights = jnp.exp2((found_of(m) - top) * FACTOR).astype(BF16)
            totals_ref[at, :] += jnp.dot(weights, with_ones(pieces[m][tokens:, :]), preferred_element_type=F32)
        out_ref[rows, cols] = divided(block, h)[0]

    @pl.when(jnp.logical_not(jnp.max(highest) < 2.0**115))
    def _():
        def one(i, _):
            at = pl.ds(pl.multiple_of(i * ROWS, ROWS), ROWS)

            @pl.when(jnp.logical_not(jnp.max(totals_ref[at, DH:]) < 2.0**115))
            def _():
                again(i // heads, i % heads, at)

            return 0

        lax.fori_loop(0, tokens // ROWS * heads, one, 0)


def local(doc_lengths, lin_q, lin_k, lin_v, log_decay, lin_gain, soft_q, soft_k, soft_v):
    doc_lengths = doc_lengths.reshape(1, -1)
    tokens = lin_q.shape[0]
    heads = lin_gain.shape[0] // DH
    count = lax.axis_size("ctx")
    bits = count.bit_length() - 1
    blocks = tokens // BLK

    head_place = lax.axis_index("head")
    own_keys, own_values = soft_k, soft_v
    for bit in range((lax.axis_size("head") // KVH).bit_length() - 1):
        far_keys, far_values = swapped((own_keys, own_values), "head", bit)
        upper = head_place // (1 << bit) % 2 == 1

        def beside(own, far):
            return jnp.where(upper, jnp.concatenate([far, own], axis=1), jnp.concatenate([own, far], axis=1))

        own_keys, own_values = beside(own_keys, far_keys), beside(own_values, far_values)
    own = jnp.concatenate([own_keys, own_values], axis=0)
    own, lin_k = lax.optimization_barrier((own, lin_k))
    pieces = [own]
    for bit in range(bits):
        pieces = pieces + [swapped(piece, "ctx", bit) for piece in pieces]
        if bit == 0:
            pieces[1], queries_later = lax.optimization_barrier((pieces[1], lin_q))

    msg_rows = heads * DH + -(-2 * heads // 16) * 16
    msg = jax.ShapeDtypeStruct((msg_rows, DH), BF16)
    total, first, sums = pl.pallas_call(
        states_kernel,
        out_shape=(
            msg,
            jax.ShapeDtypeStruct((max(blocks - 1, 1), heads * DH, DH), BF16),
            jax.ShapeDtypeStruct(log_decay.shape, F32),
        ),
        in_specs=[VMEM, HBM, HBM, VMEM],
        out_specs=(VMEM,) * 3,
        scratch_shapes=[pltpu.VMEM(lin_k.shape, BF16)] * 2 + [pltpu.SemaphoreType.DMA((2, blocks))],
        cost_estimate=lasting(2.5),
        compiler_params=within(62),
        name="states",
    )(doc_lengths, lin_k, lin_v, log_decay)

    inside = pl.pallas_call(
        inside_kernel,
        out_shape=jax.ShapeDtypeStruct(lin_q.shape, BF16),
        in_specs=[VMEM] + [VMEM] * 4,
        out_specs=VMEM,
        cost_estimate=lasting(4),
        compiler_params=within(12),
        name="inside",
    )(doc_lengths, queries_later, lin_k, lin_v, sums)

    prefix = None
    for bit in range(bits - 1):
        far = swapped(total, "ctx", bit)
        if bit == 0:
            prefix = far
        else:
            prefix = pl.pallas_call(
                functools.partial(prefix_kernel, heads, bit),
                out_shape=msg,
                in_specs=[VMEM] * 2,
                out_specs=VMEM,
                compiler_params=within(8),
        name="prefix",
            )(prefix, far)
        total = pl.pallas_call(
            functools.partial(total_kernel, heads, bit),
            out_shape=msg,
            in_specs=[VMEM] * 2,
            out_specs=VMEM,
            cost_estimate=lasting(1),
            compiler_params=within(8),
        name="total",
        )(total, far)
    far = swapped(total, "ctx", bits - 1)

    totals = jax.ShapeDtypeStruct((heads * tokens, 2 * DH), F32)
    tops = jax.ShapeDtypeStruct((heads * tokens, 128), F32)
    totals, tops = pl.pallas_call(
        near_kernel,
        out_shape=(totals, tops),
        in_specs=[VMEM, VMEM, VMEM],
        out_specs=(VMEM, VMEM),
        scratch_shapes=[pltpu.VMEM((heads * ROWS, tokens), F32)],
        compiler_params=within(20),
        cost_estimate=lasting(4),
        name="near",
    )(doc_lengths, soft_q, pieces[0])
    early = [m for m in range(2, count) if m.bit_count() == 1]
    totals = pl.pallas_call(
        functools.partial(middle_kernel, count, early),
        out_shape=totals,
        in_specs=[VMEM] + [VMEM] * (3 + len(early)),
        out_specs=VMEM,
        input_output_aliases={3: 0},
        compiler_params=within(24),
        cost_estimate=lasting(4),
        name="middle",
    )(doc_lengths, soft_q, tops, totals, *[pieces[m] for m in early])
    late = [m for m in range(1, count) if m not in early]
    soft_out, _ = pl.pallas_call(
        functools.partial(last_kernel, count, late),
        out_shape=(jax.ShapeDtypeStruct(soft_q.shape, BF16), totals),
        in_specs=[VMEM] + [VMEM] * (3 + count),
        out_specs=(VMEM, VMEM),
        input_output_aliases={3: 1},
        compiler_params=within(24),
        cost_estimate=lasting(4),
        name="last",
    )(doc_lengths, soft_q, tops, totals, *pieces)

    wide = jax.ShapeDtypeStruct(lin_q.shape, BF16)
    return pl.pallas_call(
        functools.partial(across_kernel, bits - 1),
        out_shape=(wide, wide),
        in_specs=[VMEM] * 9,
        out_specs=(HBM, HBM),
        scratch_shapes=[pltpu.VMEM(lin_q.shape, BF16), pltpu.SemaphoreType.DMA((1 + blocks,))],
        compiler_params=within(12),
        cost_estimate=lasting(3),
        name="across",
    )(doc_lengths, lin_q, inside, sums, lin_gain.reshape(1, -1), first, prefix, far, soft_out)


def solution(mesh):
    rows = P("ctx", "head")
    placed = (P(), rows, rows, rows, P("head", "ctx"), P("head"), rows, rows, rows)
    return jax.shard_map(
        local, mesh=mesh, in_specs=placed, out_specs=(rows, rows), check_vma=False
    )
```

```python
import functools

import jax
import jax.numpy as jnp
from jax import lax
from jax.experimental import pallas as pl
from jax.experimental.pallas import tpu as pltpu
from jax.sharding import PartitionSpec as P

KVH = 8
DH = 128
BLK = 256
ROWS = 256
PLACED = 90.0
LOW = -1e30
LOG2E = 1.4426950408889634
FACTOR = LOG2E * DH**-0.5
F32 = jnp.float32
BF16 = jnp.bfloat16
NT = (((1,), (1,)), ((), ()))
TN = (((0,), (0,)), ((), ()))
HBM = pl.BlockSpec(memory_space=pltpu.HBM)
VMEM = pl.BlockSpec(memory_space=pltpu.VMEM)


def within(mib):
    return pltpu.CompilerParams(vmem_limit_bytes=mib * 1024 * 1024)


def in_hbm(array):
    return pltpu.with_memory_space_constraint(array, pltpu.HBM)


def lasting(us):
    return pl.CostEstimate(flops=int(us * 0.8e9), bytes_accessed=0, transcendentals=0)


def swapped(value, axis, bit):
    return lax.ppermute(value, axis, [(i, i ^ 1 << bit) for i in range(lax.axis_size(axis))])


def bounds_of(lengths_ref):
    out, total = [], 0
    lengths = lengths_ref[...]
    for d in range(lengths.shape[1]):
        total = total + lengths[0, d]
        out.append(total)
    return out


def doc_start(bounds, position):
    start = jnp.zeros_like(position)
    for bound in bounds:
        start = jnp.where(bound <= position, bound, start)
    return start


def log_sums(decay):
    rows = lax.broadcasted_iota(jnp.int32, (BLK, BLK), 0)
    cols = lax.broadcasted_iota(jnp.int32, (BLK, BLK), 1)
    upper = jnp.where(rows <= cols, 1.0, 0.0).astype(BF16)
    found = jnp.dot(split(decay, 3).astype(BF16), upper, preferred_element_type=F32)
    count = decay.shape[0]
    return found[:count] + found[count : 2 * count] + found[2 * count :]


def split(value, count):
    terms = []
    for _ in range(count):
        term = value.astype(BF16).astype(F32)
        terms.append(term)
        value = value - term
    return jnp.concatenate(terms, axis=0)


def over_lanes(rows_form, count):
    heads = rows_form.shape[0]
    stacked = split(rows_form, count)
    extra = -stacked.shape[0] % 16
    if extra:
        stacked = jnp.concatenate([stacked, jnp.zeros((extra, stacked.shape[1]), F32)], axis=0)
    depth = stacked.shape[0]
    row = lax.broadcasted_iota(jnp.int32, (depth, heads * DH), 0)
    col = lax.broadcasted_iota(jnp.int32, (depth, heads * DH), 1)
    picks = jnp.where((row % heads == col // DH) & (row < count * heads), 1.0, 0.0).astype(BF16)
    return lax.dot_general(stacked.astype(BF16), picks, TN, preferred_element_type=F32)


def fetch_kernel(keys, values, decay, lengths, own_ref, decay_ref, lengths_ref, sems):
    tokens = keys.shape[0]
    pairs = [
        (keys, own_ref.at[pl.ds(0, tokens), :]),
        (values, own_ref.at[pl.ds(tokens, tokens), :]),
        (decay, decay_ref),
        (lengths, lengths_ref),
    ]
    copies = [pltpu.make_async_copy(a, b, sems.at[i]) for i, (a, b) in enumerate(pairs)]
    for copy in copies:
        copy.start()
    for copy in copies:
        copy.wait()


def states_kernel(lengths_ref, keys_hbm, values_hbm, decay_ref, msg_ref, first_ref, sums_ref, keys_ref, values_ref, sems):
    heads = decay_ref.shape[0]
    tokens = keys_ref.shape[0]
    base = lax.axis_index("ctx") * tokens
    bounds = bounds_of(lengths_ref)
    place = lax.broadcasted_iota(jnp.int32, (1, BLK), 1)
    blocks = tokens // BLK
    copies = []
    for b in range(blocks):
        rows = slice(b * BLK, (b + 1) * BLK)
        copies.append(pltpu.make_async_copy(keys_hbm.at[rows, :], keys_ref.at[rows, :], sems.at[0, b]))
        copies.append(pltpu.make_async_copy(values_hbm.at[rows, :], values_ref.at[rows, :], sems.at[1, b]))
    for copy in copies:
        copy.start()
    through = jnp.ones((heads, 1), F32)
    weights, factors = [], []
    for b in range(blocks):
        s = base + b * BLK
        start_last = doc_start(bounds, s + BLK - 1)
        kept = jnp.where(start_last < s, 1.0, 0.0).astype(F32)
        sums = log_sums(decay_ref[:, b * BLK : (b + 1) * BLK])
        sums_ref[:, b * BLK : (b + 1) * BLK] = sums
        closing = sums[:, BLK - 1 : BLK]
        weight = jnp.where(s + place >= start_last, jnp.exp(closing - sums), 0.0)
        weights.append(over_lanes(weight, 2))
        factors.append(kept * jnp.exp(closing))
        through = through * factors[b]
    state = [None] * heads
    for b in range(blocks):
        copies[2 * b].wait()
        copies[2 * b + 1].wait()
        rows = slice(b * BLK, (b + 1) * BLK)
        for h in range(heads):
            cols = slice(h * DH, (h + 1) * DH)
            weighted = (keys_ref[rows, cols].astype(F32) * weights[b][:, cols]).astype(BF16)
            update = lax.dot_general(weighted, values_ref[rows, cols], TN, preferred_element_type=F32)
            state[h] = update if b == 0 else factors[b][h : h + 1, :] * state[h] + update
            if b < blocks - 1:
                first_ref[b, cols, :] = update.astype(BF16)
    for h in range(heads):
        msg_ref[h * DH : (h + 1) * DH, :] = state[h].astype(BF16)
    tail = jnp.broadcast_to(split(through, 2), (2 * heads, DH))
    extra = msg_ref.shape[0] - heads * DH - 2 * heads
    if extra:
        tail = jnp.concatenate([tail, jnp.zeros((extra, DH), F32)], axis=0)
    msg_ref[heads * DH :, :] = tail.astype(BF16)


def inside_kernel(lengths_ref, queries_ref, keys_ref, values_ref, sums_ref, out_ref, entering_ref):
    heads = sums_ref.shape[0]
    tokens = keys_ref.shape[0]
    base = lax.axis_index("ctx") * tokens
    bounds = bounds_of(lengths_ref)
    rows = lax.broadcasted_iota(jnp.int32, (BLK, BLK), 0)
    cols = lax.broadcasted_iota(jnp.int32, (BLK, BLK), 1)
    place = lax.broadcasted_iota(jnp.int32, (BLK, 1), 0)
    across = lax.broadcasted_iota(jnp.int32, (1, BLK), 1)
    for b in range(tokens // BLK):
        s = base + b * BLK
        start = doc_start(bounds, s + place) - s
        bias = jnp.where((cols <= rows) & (cols >= start), 0.0, LOW)
        here = slice(b * BLK, (b + 1) * BLK)
        sums = sums_ref[:, here] * LOG2E
        down = over_lanes(sums, 3)
        entering = jnp.where(doc_start(bounds, s + across) < s, jnp.exp2(sums), 0.0)
        entering_ref[here, :] = over_lanes(entering, 2)
        for h in range(heads):
            there = slice(h * DH, (h + 1) * DH)
            upright = jnp.concatenate([down[:, there]] * (BLK // DH), axis=1)
            spread = upright - sums[h : h + 1, :] + bias
            scores = lax.dot_general(
                queries_ref[here, there], keys_ref[here, there], NT, preferred_element_type=F32
            )
            scores = (scores * jnp.exp2(spread)).astype(BF16)
            out_ref[here, there] = jnp.dot(
                scores, values_ref[here, there], preferred_element_type=F32
            ).astype(BF16)


def through_of(msg_ref, heads, h):
    high = msg_ref[heads * DH + h : heads * DH + h + 1, :].astype(F32)
    low = msg_ref[heads * DH + heads + h : heads * DH + heads + h + 1, :].astype(F32)
    return high + low


def joined(heads, early_ref, late_ref, swap, out_ref):
    def pick(here):
        one, two = early_ref[here, :].astype(F32), late_ref[here, :].astype(F32)
        return jnp.where(swap, two, one), jnp.where(swap, one, two)

    def through(h):
        high = pick(slice(heads * DH + h, heads * DH + h + 1))
        low = pick(slice(heads * DH + heads + h, heads * DH + heads + h + 1))
        return high[0] + low[0], high[1] + low[1]

    tails = []
    for h in range(heads):
        here = slice(h * DH, (h + 1) * DH)
        early, late = pick(here)
        early_through, late_through = through(h)
        out_ref[here, :] = (late_through * early + late).astype(BF16)
        tails.append(late_through * early_through)
    tail = jnp.concatenate(tails, axis=0)
    high = tail.astype(BF16).astype(F32)
    pieces = [high, tail - high]
    extra = out_ref.shape[0] - heads * DH - 2 * heads
    if extra:
        pieces.append(jnp.zeros((extra, DH), F32))
    out_ref[heads * DH :, :] = jnp.concatenate(pieces, axis=0).astype(BF16)


def upper_half(bit):
    return (lax.axis_index("ctx") // (1 << bit)) % 2 == 1


def total_kernel(heads, bit, total_ref, far_ref, new_total_ref):
    joined(heads, total_ref, far_ref, upper_half(bit), new_total_ref)


def prefix_kernel(heads, bit, prefix_ref, far_ref, new_prefix_ref):
    if bit == 1:
        first = jnp.where(upper_half(0), 1.0, 0.0).astype(F32)
        rows = prefix_ref.shape[0]
        tail = lax.broadcasted_iota(jnp.int32, (rows, DH), 0) - heads * DH
        own = prefix_ref[...].astype(F32) * first
        neutral = jnp.where((tail >= 0) & (tail < heads), 1.0 - first, 0.0)
        prefix_ref = (own + neutral).astype(BF16)

    @pl.when(upper_half(bit))
    def _():
        joined(heads, far_ref, prefix_ref, False, new_prefix_ref)

    @pl.when(jnp.logical_not(upper_half(bit)))
    def _():
        new_prefix_ref[...] = prefix_ref[...]


def across_kernel(
    bit, lengths_ref, queries_ref, inside_ref, entering_ref, sums_ref, gain_ref, first_ref, prefix_ref, far_ref, soft_ref,
    out_hbm, soft_hbm, out_ref, sems,
):
    soft_copy = pltpu.make_async_copy(soft_ref, soft_hbm, sems.at[0])
    soft_copy.start()
    copies = []
    heads = sums_ref.shape[0]
    tokens = queries_ref.shape[0]
    place_ctx = lax.axis_index("ctx")
    base = place_ctx * tokens
    upper = jnp.where(upper_half(bit), 1.0, 0.0).astype(F32)
    valid = jnp.where(upper_half(0), 1.0, 0.0).astype(F32) if bit == 1 else 1.0
    bounds = bounds_of(lengths_ref)
    state = []
    for h in range(heads):
        here = slice(h * DH, (h + 1) * DH)
        through = upper * (valid * through_of(prefix_ref, heads, h) + (1.0 - valid))
        state.append(valid * prefix_ref[here, :].astype(F32) + through * far_ref[here, :].astype(F32))
    pair = 2 * DH
    row = lax.broadcasted_iota(jnp.int32, (pair, pair), 0)
    col = lax.broadcasted_iota(jnp.int32, (pair, pair), 1)
    ones = jnp.where(row // DH == col // DH, 1.0, 0.0).astype(BF16)
    zeros = jnp.zeros((DH, DH), BF16)
    for b in range(tokens // BLK):
        s = base + b * BLK
        here = slice(b * BLK, (b + 1) * BLK)
        start_last = doc_start(bounds, s + BLK - 1)
        kept = jnp.where(start_last < s, 1.0, 0.0).astype(F32)
        factor = kept * jnp.exp(sums_ref[:, (b + 1) * BLK - 1 : (b + 1) * BLK])
        for h in range(0, heads, 2):
            there = slice(h * DH, (h + 2) * DH)
            left = jnp.concatenate([state[h].astype(BF16), zeros], axis=1)
            right = jnp.concatenate([zeros, state[h + 1].astype(BF16)], axis=1)
            across = jnp.dot(
                queries_ref[here, there],
                jnp.concatenate([left, right], axis=0),
                preferred_element_type=F32,
            )
            raw = inside_ref[here, there].astype(F32) + across * entering_ref[here, there]
            square = jnp.dot((raw * raw).astype(BF16), ones, preferred_element_type=F32)
            scale = lax.rsqrt(square * (1.0 / DH) + 1e-06)
            out_ref[here, there] = (raw * scale * gain_ref[:, there]).astype(BF16)
            if b < tokens // BLK - 1:
                for one in (h, h + 1):
                    update = first_ref[b, one * DH : (one + 1) * DH, :].astype(F32)
                    state[one] = factor[one : one + 1, :] * state[one] + update
        copies.append(pltpu.make_async_copy(out_ref.at[here, :], out_hbm.at[here, :], sems.at[1 + b]))
        copies[b].start()
    soft_copy.wait()
    for copy in copies:
        copy.wait()


def origin_of(m, count):
    place = lax.axis_index("ctx")
    origin = jnp.int32(0)
    bit = 1
    while bit < count:
        mine = (place // bit) % 2
        origin = origin + bit * (1 - mine if m & bit else mine)
        bit *= 2
    return origin


def bias_of(bounds, first_row, rows, first_key, count):
    row = first_row + lax.broadcasted_iota(jnp.int32, (rows, 1), 0)
    key = first_key + lax.broadcasted_iota(jnp.int32, (rows, count), 1)
    return jnp.where((key >= doc_start(bounds, row)) & (key <= row), 0.0, LOW)


def with_ones(values):
    return jnp.concatenate([values, jnp.ones(values.shape, BF16)], axis=1)


def weighted(found, top):
    spread = [found[:, p : p + 128] * FACTOR - top for p in range(0, found.shape[1], 128)]
    return jnp.concatenate([jnp.exp2(x).astype(BF16) for x in spread], axis=1)


def near_kernel(lengths_ref, queries_ref, own_ref, totals_ref, tops_ref, scores):
    tokens = queries_ref.shape[0]
    heads = queries_ref.shape[1] // DH
    base = lax.axis_index("ctx") * tokens
    bounds = bounds_of(lengths_ref)
    for block in range(tokens // ROWS):
        count = (block + 1) * ROWS
        rows = slice(block * ROWS, (block + 1) * ROWS)
        bias = bias_of(bounds, base + block * ROWS, ROWS, base, count)
        key, value = own_ref[:count, :], with_ones(own_ref[tokens : tokens + count, :])
        for h in range(heads):
            there = slice(h * ROWS, (h + 1) * ROWS)
            at = slice((block * heads + h) * ROWS, (block * heads + h + 1) * ROWS)
            found = lax.dot_general(
                queries_ref[rows, h * DH : (h + 1) * DH], key, NT, preferred_element_type=F32
            )
            found = found + bias
            scores[there, :count] = found
            top = found[:, :128]
            for p in range(128, count, 128):
                top = jnp.maximum(top, found[:, p : p + 128])
            top = jnp.max(top, axis=1, keepdims=True) * FACTOR + PLACED
            tops_ref[at, :] = jnp.broadcast_to(top, (ROWS, 128))
        for h in range(heads):
            there = slice(h * ROWS, (h + 1) * ROWS)
            at = slice((block * heads + h) * ROWS, (block * heads + h + 1) * ROWS)
            totals_ref[at, :] = jnp.dot(
                weighted(scores[there, :count], tops_ref[at, :]), value, preferred_element_type=F32
            )


def add_piece(bounds, base, block, origin, queries_ref, piece_ref, totals_ref, tops_ref):
    tokens = queries_ref.shape[0]
    heads = queries_ref.shape[1] // DH
    s = base + block * ROWS
    first = origin * tokens
    needed = (first < base) & (first + tokens > doc_start(bounds, s))
    whole = first >= doc_start(bounds, s + ROWS - 1)
    half = first + tokens <= doc_start(bounds, s + ROWS // 2)

    def add(bias, rows):
        key, value = piece_ref[:tokens, :], with_ones(piece_ref[tokens:, :])
        for h in range(heads):
            at = pl.ds(pl.multiple_of((block * heads + h) * ROWS, ROWS), rows)
            query = queries_ref[pl.ds(pl.multiple_of(block * ROWS, ROWS), rows), h * DH : (h + 1) * DH]
            found = lax.dot_general(query, key, NT, preferred_element_type=F32)
            if bias is not None:
                found = found + bias
            totals_ref[at, :] += jnp.dot(weighted(found, tops_ref[at, :]), value, preferred_element_type=F32)

    @pl.when(needed & whole)
    def _():
        add(None, ROWS)

    @pl.when(needed & jnp.logical_not(whole) & jnp.logical_not(half))
    def _():
        add(bias_of(bounds, s, ROWS, first, tokens), ROWS)

    @pl.when(needed & half)
    def _():
        add(bias_of(bounds, s, ROWS // 2, first, tokens), ROWS // 2)


def middle_kernel(count, which, block, lengths_ref, queries_ref, tops_ref, totals_in, *refs):
    pieces, totals_ref = refs[:-1], refs[-1]
    tokens = queries_ref.shape[0]
    base = lax.axis_index("ctx") * tokens
    bounds = bounds_of(lengths_ref)

    for m, piece in zip(which, pieces):
        add_piece(bounds, base, block, origin_of(m, count), queries_ref, piece, totals_ref, tops_ref)


def last_kernel(count, which, lengths_ref, queries_ref, tops_ref, totals_in, *refs):
    pieces, out_ref, totals_ref = refs[:count], refs[count], refs[count + 1]
    tokens = queries_ref.shape[0]
    heads = queries_ref.shape[1] // DH
    base = lax.axis_index("ctx") * tokens
    bounds = bounds_of(lengths_ref)

    def row_block(block, _):
        for m in which:
            add_piece(bounds, base, block, origin_of(m, count), queries_ref, pieces[m], totals_ref, tops_ref)
        return 0

    lax.fori_loop(0, tokens // ROWS, row_block, 0)

    def divided(block, h):
        at = pl.ds(pl.multiple_of((block * heads + h) * ROWS, ROWS), ROWS)
        total = totals_ref[at, DH:]
        return (totals_ref[at, :DH] * pl.reciprocal(total, approx=True)).astype(BF16), total

    highest = jnp.zeros((ROWS, DH), F32)
    for block in range(tokens // ROWS):
        for h in range(heads):
            found, total = divided(block, h)
            out_ref[block * ROWS : (block + 1) * ROWS, h * DH : (h + 1) * DH] = found
            highest = jnp.maximum(highest, total)

    def again(block, h, at):
        s = base + block * ROWS
        rows = pl.ds(pl.multiple_of(block * ROWS, ROWS), ROWS)
        cols = pl.ds(pl.multiple_of(h * DH, DH), DH)
        query = queries_ref[rows, cols]

        def found_of(m):
            found = lax.dot_general(query, pieces[m][:tokens, :], NT, preferred_element_type=F32)
            return found + bias_of(bounds, s, ROWS, origin_of(m, count) * tokens, tokens)

        top = jnp.full((ROWS, 1), LOW, F32)
        for m in range(count):
            top = jnp.maximum(top, jnp.max(found_of(m), axis=1, keepdims=True))
        totals_ref[at, :] = jnp.zeros((ROWS, 2 * DH), F32)
        for m in range(count):
            weights = jnp.exp2((found_of(m) - top) * FACTOR).astype(BF16)
            totals_ref[at, :] += jnp.dot(weights, with_ones(pieces[m][tokens:, :]), preferred_element_type=F32)
        out_ref[rows, cols] = divided(block, h)[0]

    @pl.when(jnp.logical_not(jnp.max(highest) < 2.0**115))
    def _():
        def one(i, _):
            at = pl.ds(pl.multiple_of(i * ROWS, ROWS), ROWS)

            @pl.when(jnp.logical_not(jnp.max(totals_ref[at, DH:]) < 2.0**115))
            def _():
                again(i // heads, i % heads, at)

            return 0

        lax.fori_loop(0, tokens // ROWS * heads, one, 0)


def local(doc_lengths, lin_q, lin_k, lin_v, log_decay, lin_gain, soft_q, soft_k, soft_v):
    doc_lengths = doc_lengths.reshape(1, -1)
    tokens = lin_q.shape[0]
    heads = lin_gain.shape[0] // DH
    count = lax.axis_size("ctx")
    bits = count.bit_length() - 1
    blocks = tokens // BLK

    head_place = lax.axis_index("head")
    own_keys, own_values = soft_k, soft_v
    for bit in range((lax.axis_size("head") // KVH).bit_length() - 1):
        far_keys, far_values = swapped((own_keys, own_values), "head", bit)
        upper = head_place // (1 << bit) % 2 == 1

        def beside(own, far):
            return jnp.where(upper, jnp.concatenate([far, own], axis=1), jnp.concatenate([own, far], axis=1))

        own_keys, own_values = beside(own_keys, far_keys), beside(own_values, far_values)
    own, log_decay, doc_lengths = pl.pallas_call(
        fetch_kernel,
        out_shape=(
            pltpu.VMEM((2 * tokens, DH), BF16),
            pltpu.VMEM(log_decay.shape, F32),
            pltpu.VMEM(doc_lengths.shape, jnp.int32),
        ),
        in_specs=[HBM] * 4,
        out_specs=(VMEM,) * 3,
        scratch_shapes=[pltpu.SemaphoreType.DMA((4,))],
        compiler_params=within(2),
        cost_estimate=lasting(1),
        name="fetch",
    )(in_hbm(own_keys), in_hbm(own_values), in_hbm(log_decay), in_hbm(doc_lengths))
    own, lin_k = lax.optimization_barrier((own, lin_k))
    pieces = [own]
    for bit in range(bits):
        pieces = pieces + [swapped(piece, "ctx", bit) for piece in pieces]
        if bit == 0:
            pieces[1], queries_later = lax.optimization_barrier((pieces[1], lin_q))

    msg_rows = heads * DH + -(-2 * heads // 16) * 16
    msg = jax.ShapeDtypeStruct((msg_rows, DH), BF16)
    total, first, sums = pl.pallas_call(
        states_kernel,
        out_shape=(
            pltpu.VMEM(msg.shape, BF16),
            pltpu.VMEM((max(blocks - 1, 1), heads * DH, DH), BF16),
            pltpu.VMEM(log_decay.shape, F32),
        ),
        in_specs=[VMEM, HBM, HBM, VMEM],
        out_specs=(VMEM,) * 3,
        scratch_shapes=[pltpu.VMEM(lin_k.shape, BF16)] * 2 + [pltpu.SemaphoreType.DMA((2, blocks))],
        cost_estimate=lasting(2.5),
        compiler_params=within(12),
        name="states",
    )(doc_lengths, in_hbm(lin_k), in_hbm(lin_v), log_decay)

    totals = jax.ShapeDtypeStruct((heads * tokens, 2 * DH), F32)
    tops = jax.ShapeDtypeStruct((heads * tokens, 128), F32)
    totals, tops = pl.pallas_call(
        near_kernel,
        out_shape=(totals, tops),
        in_specs=[VMEM, VMEM, VMEM],
        out_specs=(VMEM, VMEM),
        scratch_shapes=[pltpu.VMEM((heads * ROWS, tokens), F32)],
        compiler_params=within(20),
        cost_estimate=lasting(4),
        name="near",
    )(doc_lengths, soft_q, pieces[0])
    total, tops = lax.optimization_barrier((total, tops))

    inside, entering = pl.pallas_call(
        inside_kernel,
        out_shape=(pltpu.VMEM(lin_q.shape, BF16), pltpu.VMEM(lin_q.shape, F32)),
        in_specs=[VMEM] + [VMEM] * 4,
        out_specs=(VMEM, VMEM),
        cost_estimate=lasting(4),
        compiler_params=within(12),
        name="inside",
    )(doc_lengths, queries_later, lin_k, lin_v, sums)

    prefix = None
    for bit in range(bits - 1):
        far = swapped(total, "ctx", bit)
        if bit == 0:
            prefix = far
        else:
            prefix = pl.pallas_call(
                functools.partial(prefix_kernel, heads, bit),
                out_shape=msg,
                in_specs=[VMEM] * 2,
                out_specs=VMEM,
                compiler_params=within(8),
        name="prefix",
            )(prefix, far)
        total = pl.pallas_call(
            functools.partial(total_kernel, heads, bit),
            out_shape=msg,
            in_specs=[VMEM] * 2,
            out_specs=VMEM,
            cost_estimate=lasting(1),
            compiler_params=within(8),
        name="total",
        )(total, far)

    early = [m for m in range(2, count) if m.bit_count() == 1]
    def middle(block, totals):
        return pl.pallas_call(
            functools.partial(middle_kernel, count, early, block),
            out_shape=jax.ShapeDtypeStruct(totals.shape, F32),
            in_specs=[VMEM] + [VMEM] * (3 + len(early)),
            out_specs=VMEM,
            input_output_aliases={3: 0},
            compiler_params=within(24),
            cost_estimate=lasting(2),
            name="middle",
        )(doc_lengths, soft_q, tops, totals, *[pieces[m] for m in early])

    steps = tokens // ROWS
    for block in range(steps // 2):
        totals = middle(block, totals)
    total, totals = lax.optimization_barrier((total, totals))
    far = swapped(total, "ctx", bits - 1)
    for block in range(steps // 2, steps):
        totals = middle(block, totals)
    late = [m for m in range(1, count) if m not in early]
    soft_out, _ = pl.pallas_call(
        functools.partial(last_kernel, count, late),
        out_shape=(jax.ShapeDtypeStruct(soft_q.shape, BF16), jax.ShapeDtypeStruct(totals.shape, F32)),
        in_specs=[VMEM] + [VMEM] * (3 + count),
        out_specs=(VMEM, VMEM),
        input_output_aliases={3: 1},
        compiler_params=within(24),
        cost_estimate=lasting(4),
        name="last",
    )(doc_lengths, soft_q, tops, totals, *pieces)

    wide = jax.ShapeDtypeStruct(lin_q.shape, BF16)
    return pl.pallas_call(
        functools.partial(across_kernel, bits - 1),
        out_shape=(wide, wide),
        in_specs=[VMEM] * 10,
        out_specs=(HBM, HBM),
        scratch_shapes=[pltpu.VMEM(lin_q.shape, BF16), pltpu.SemaphoreType.DMA((1 + blocks,))],
        compiler_params=within(12),
        cost_estimate=lasting(3),
        name="across",
    )(doc_lengths, lin_q, inside, entering, sums, lin_gain.reshape(1, -1), first, prefix, far, soft_out)


def solution(mesh):
    rows = P("ctx", "head")
    placed = (P(), rows, rows, rows, P("head", "ctx"), P("head"), rows, rows, rows)
    return jax.shard_map(
        local, mesh=mesh, in_specs=placed, out_specs=(rows, rows), check_vma=False
    )
```

```python
import functools

import jax
import jax.numpy as jnp
from jax import lax
from jax.experimental import pallas as pl
from jax.experimental.pallas import tpu as pltpu
from jax.sharding import PartitionSpec as P

KVH = 8
DH = 128
BLK = 256
ROWS = 256
PLACED = 90.0
LOW = -1e30
LOG2E = 1.4426950408889634
FACTOR = LOG2E * DH**-0.5
F32 = jnp.float32
BF16 = jnp.bfloat16
NT = (((1,), (1,)), ((), ()))
TN = (((0,), (0,)), ((), ()))
HBM = pl.BlockSpec(memory_space=pltpu.HBM)
VMEM = pl.BlockSpec(memory_space=pltpu.VMEM)


def within(mib):
    return pltpu.CompilerParams(vmem_limit_bytes=mib * 1024 * 1024)


def in_hbm(array):
    return pltpu.with_memory_space_constraint(array, pltpu.HBM)


def lasting(us):
    return pl.CostEstimate(flops=int(us * 0.8e9), bytes_accessed=0, transcendentals=0)


def swapped(value, axis, bit):
    return lax.ppermute(value, axis, [(i, i ^ 1 << bit) for i in range(lax.axis_size(axis))])


def bounds_of(lengths_ref):
    out, total = [], 0
    lengths = lengths_ref[...]
    for d in range(lengths.shape[1]):
        total = total + lengths[0, d]
        out.append(total)
    return out


def doc_start(bounds, position):
    start = jnp.zeros_like(position)
    for bound in bounds:
        start = jnp.where(bound <= position, bound, start)
    return start


def log_sums(decay):
    rows = lax.broadcasted_iota(jnp.int32, (BLK, BLK), 0)
    cols = lax.broadcasted_iota(jnp.int32, (BLK, BLK), 1)
    upper = jnp.where(rows <= cols, 1.0, 0.0).astype(BF16)
    found = jnp.dot(split(decay, 3).astype(BF16), upper, preferred_element_type=F32)
    count = decay.shape[0]
    return found[:count] + found[count : 2 * count] + found[2 * count :]


def split(value, count):
    terms = []
    for _ in range(count):
        term = value.astype(BF16).astype(F32)
        terms.append(term)
        value = value - term
    return jnp.concatenate(terms, axis=0)


def over_lanes(rows_form, count):
    heads = rows_form.shape[0]
    stacked = split(rows_form, count)
    extra = -stacked.shape[0] % 16
    if extra:
        stacked = jnp.concatenate([stacked, jnp.zeros((extra, stacked.shape[1]), F32)], axis=0)
    depth = stacked.shape[0]
    row = lax.broadcasted_iota(jnp.int32, (depth, heads * DH), 0)
    col = lax.broadcasted_iota(jnp.int32, (depth, heads * DH), 1)
    picks = jnp.where((row % heads == col // DH) & (row < count * heads), 1.0, 0.0).astype(BF16)
    return lax.dot_general(stacked.astype(BF16), picks, TN, preferred_element_type=F32)


def fetch_kernel(keys, values, decay, lengths, own_ref, decay_ref, lengths_ref, sems):
    tokens = keys.shape[0]
    pairs = [
        (keys, own_ref.at[pl.ds(0, tokens), :]),
        (values, own_ref.at[pl.ds(tokens, tokens), :]),
        (decay, decay_ref),
        (lengths, lengths_ref),
    ]
    copies = [pltpu.make_async_copy(a, b, sems.at[i]) for i, (a, b) in enumerate(pairs)]
    for copy in copies:
        copy.start()
    for copy in copies:
        copy.wait()


def states_kernel(lengths_ref, keys_hbm, values_hbm, decay_ref, msg_ref, first_ref, sums_ref, keys_ref, values_ref, sems):
    heads = decay_ref.shape[0]
    tokens = keys_ref.shape[0]
    base = lax.axis_index("ctx") * tokens
    bounds = bounds_of(lengths_ref)
    place = lax.broadcasted_iota(jnp.int32, (1, BLK), 1)
    blocks = tokens // BLK
    copies = []
    for b in range(blocks):
        rows = slice(b * BLK, (b + 1) * BLK)
        copies.append(pltpu.make_async_copy(keys_hbm.at[rows, :], keys_ref.at[rows, :], sems.at[0, b]))
        copies.append(pltpu.make_async_copy(values_hbm.at[rows, :], values_ref.at[rows, :], sems.at[1, b]))
    for copy in copies:
        copy.start()
    through = jnp.ones((heads, 1), F32)
    weights, factors = [], []
    for b in range(blocks):
        s = base + b * BLK
        start_last = doc_start(bounds, s + BLK - 1)
        kept = jnp.where(start_last < s, 1.0, 0.0).astype(F32)
        sums = log_sums(decay_ref[:, b * BLK : (b + 1) * BLK])
        sums_ref[:, b * BLK : (b + 1) * BLK] = sums
        closing = sums[:, BLK - 1 : BLK]
        weight = jnp.where(s + place >= start_last, jnp.exp(closing - sums), 0.0)
        weights.append(over_lanes(weight, 2))
        factors.append(kept * jnp.exp(closing))
        through = through * factors[b]
    state = [None] * heads
    for b in range(blocks):
        copies[2 * b].wait()
        copies[2 * b + 1].wait()
        rows = slice(b * BLK, (b + 1) * BLK)
        for h in range(heads):
            cols = slice(h * DH, (h + 1) * DH)
            weighted = (keys_ref[rows, cols].astype(F32) * weights[b][:, cols]).astype(BF16)
            update = lax.dot_general(weighted, values_ref[rows, cols], TN, preferred_element_type=F32)
            state[h] = update if b == 0 else factors[b][h : h + 1, :] * state[h] + update
            if b < blocks - 1:
                first_ref[b, cols, :] = update.astype(BF16)
    for h in range(heads):
        msg_ref[h * DH : (h + 1) * DH, :] = state[h].astype(BF16)
    tail = jnp.broadcast_to(split(through, 2), (2 * heads, DH))
    extra = msg_ref.shape[0] - heads * DH - 2 * heads
    if extra:
        tail = jnp.concatenate([tail, jnp.zeros((extra, DH), F32)], axis=0)
    msg_ref[heads * DH :, :] = tail.astype(BF16)


def inside_kernel(lengths_ref, queries_ref, keys_ref, values_ref, sums_ref, out_ref, entering_ref):
    heads = sums_ref.shape[0]
    tokens = keys_ref.shape[0]
    base = lax.axis_index("ctx") * tokens
    bounds = bounds_of(lengths_ref)
    rows = lax.broadcasted_iota(jnp.int32, (BLK, BLK), 0)
    cols = lax.broadcasted_iota(jnp.int32, (BLK, BLK), 1)
    place = lax.broadcasted_iota(jnp.int32, (BLK, 1), 0)
    across = lax.broadcasted_iota(jnp.int32, (1, BLK), 1)
    for b in range(tokens // BLK):
        s = base + b * BLK
        start = doc_start(bounds, s + place) - s
        bias = jnp.where((cols <= rows) & (cols >= start), 0.0, LOW)
        here = slice(b * BLK, (b + 1) * BLK)
        sums = sums_ref[:, here] * LOG2E
        down = over_lanes(sums, 3)
        entering = jnp.where(doc_start(bounds, s + across) < s, jnp.exp2(sums), 0.0)
        entering_ref[here, :] = over_lanes(entering, 2)
        for h in range(heads):
            there = slice(h * DH, (h + 1) * DH)
            upright = jnp.concatenate([down[:, there]] * (BLK // DH), axis=1)
            spread = upright - sums[h : h + 1, :] + bias
            scores = lax.dot_general(
                queries_ref[here, there], keys_ref[here, there], NT, preferred_element_type=F32
            )
            scores = (scores * jnp.exp2(spread)).astype(BF16)
            out_ref[here, there] = jnp.dot(
                scores, values_ref[here, there], preferred_element_type=F32
            ).astype(BF16)


def through_of(msg_ref, heads, h):
    high = msg_ref[heads * DH + h : heads * DH + h + 1, :].astype(F32)
    low = msg_ref[heads * DH + heads + h : heads * DH + heads + h + 1, :].astype(F32)
    return high + low


def joined(heads, early_ref, late_ref, swap, out_ref):
    def pick(here):
        one, two = early_ref[here, :].astype(F32), late_ref[here, :].astype(F32)
        return jnp.where(swap, two, one), jnp.where(swap, one, two)

    def through(h):
        high = pick(slice(heads * DH + h, heads * DH + h + 1))
        low = pick(slice(heads * DH + heads + h, heads * DH + heads + h + 1))
        return high[0] + low[0], high[1] + low[1]

    tails = []
    for h in range(heads):
        here = slice(h * DH, (h + 1) * DH)
        early, late = pick(here)
        early_through, late_through = through(h)
        out_ref[here, :] = (late_through * early + late).astype(BF16)
        tails.append(late_through * early_through)
    tail = jnp.concatenate(tails, axis=0)
    high = tail.astype(BF16).astype(F32)
    pieces = [high, tail - high]
    extra = out_ref.shape[0] - heads * DH - 2 * heads
    if extra:
        pieces.append(jnp.zeros((extra, DH), F32))
    out_ref[heads * DH :, :] = jnp.concatenate(pieces, axis=0).astype(BF16)


def upper_half(bit):
    return (lax.axis_index("ctx") // (1 << bit)) % 2 == 1


def total_kernel(heads, bit, total_ref, far_ref, new_total_ref):
    joined(heads, total_ref, far_ref, upper_half(bit), new_total_ref)


def prefix_kernel(heads, bit, prefix_ref, far_ref, new_prefix_ref):
    if bit == 1:
        first = jnp.where(upper_half(0), 1.0, 0.0).astype(F32)
        rows = prefix_ref.shape[0]
        tail = lax.broadcasted_iota(jnp.int32, (rows, DH), 0) - heads * DH
        own = prefix_ref[...].astype(F32) * first
        neutral = jnp.where((tail >= 0) & (tail < heads), 1.0 - first, 0.0)
        prefix_ref = (own + neutral).astype(BF16)

    @pl.when(upper_half(bit))
    def _():
        joined(heads, far_ref, prefix_ref, False, new_prefix_ref)

    @pl.when(jnp.logical_not(upper_half(bit)))
    def _():
        new_prefix_ref[...] = prefix_ref[...]


def across_kernel(
    bit, lengths_ref, queries_ref, inside_ref, entering_ref, sums_ref, gain_ref, first_ref, prefix_ref, far_ref, soft_ref,
    out_hbm, soft_hbm, out_ref, sems,
):
    soft_copy = pltpu.make_async_copy(soft_ref, soft_hbm, sems.at[0])
    soft_copy.start()
    copies = []
    heads = sums_ref.shape[0]
    tokens = queries_ref.shape[0]
    place_ctx = lax.axis_index("ctx")
    base = place_ctx * tokens
    upper = jnp.where(upper_half(bit), 1.0, 0.0).astype(F32)
    valid = jnp.where(upper_half(0), 1.0, 0.0).astype(F32) if bit == 1 else 1.0
    bounds = bounds_of(lengths_ref)
    state = []
    for h in range(heads):
        here = slice(h * DH, (h + 1) * DH)
        through = upper * (valid * through_of(prefix_ref, heads, h) + (1.0 - valid))
        state.append(valid * prefix_ref[here, :].astype(F32) + through * far_ref[here, :].astype(F32))
    pair = 2 * DH
    row = lax.broadcasted_iota(jnp.int32, (pair, pair), 0)
    col = lax.broadcasted_iota(jnp.int32, (pair, pair), 1)
    ones = jnp.where(row // DH == col // DH, 1.0, 0.0).astype(BF16)
    zeros = jnp.zeros((DH, DH), BF16)
    for b in range(tokens // BLK):
        s = base + b * BLK
        here = slice(b * BLK, (b + 1) * BLK)
        start_last = doc_start(bounds, s + BLK - 1)
        kept = jnp.where(start_last < s, 1.0, 0.0).astype(F32)
        factor = kept * jnp.exp(sums_ref[:, (b + 1) * BLK - 1 : (b + 1) * BLK])
        for h in range(0, heads, 2):
            there = slice(h * DH, (h + 2) * DH)
            left = jnp.concatenate([state[h].astype(BF16), zeros], axis=1)
            right = jnp.concatenate([zeros, state[h + 1].astype(BF16)], axis=1)
            across = jnp.dot(
                queries_ref[here, there],
                jnp.concatenate([left, right], axis=0),
                preferred_element_type=F32,
            )
            raw = inside_ref[here, there].astype(F32) + across * entering_ref[here, there]
            square = jnp.dot((raw * raw).astype(BF16), ones, preferred_element_type=F32)
            scale = lax.rsqrt(square * (1.0 / DH) + 1e-06)
            out_ref[here, there] = (raw * scale * gain_ref[:, there]).astype(BF16)
            if b < tokens // BLK - 1:
                for one in (h, h + 1):
                    update = first_ref[b, one * DH : (one + 1) * DH, :].astype(F32)
                    state[one] = factor[one : one + 1, :] * state[one] + update
        copies.append(pltpu.make_async_copy(out_ref.at[here, :], out_hbm.at[here, :], sems.at[1 + b]))
        copies[b].start()
    soft_copy.wait()
    for copy in copies:
        copy.wait()


def origin_of(m, count):
    place = lax.axis_index("ctx")
    origin = jnp.int32(0)
    bit = 1
    while bit < count:
        mine = (place // bit) % 2
        origin = origin + bit * (1 - mine if m & bit else mine)
        bit *= 2
    return origin


def bias_of(bounds, first_row, rows, first_key, count):
    row = first_row + lax.broadcasted_iota(jnp.int32, (rows, 1), 0)
    key = first_key + lax.broadcasted_iota(jnp.int32, (rows, count), 1)
    return jnp.where((key >= doc_start(bounds, row)) & (key <= row), 0.0, LOW)


def with_ones(values):
    return jnp.concatenate([values, jnp.ones(values.shape, BF16)], axis=1)


def weighted(found, top):
    spread = [found[:, p : p + 128] * FACTOR - top for p in range(0, found.shape[1], 128)]
    return jnp.concatenate([jnp.exp2(x).astype(BF16) for x in spread], axis=1)


def near_kernel(lengths_ref, queries_ref, own_ref, totals_ref, tops_ref, scores):
    tokens = queries_ref.shape[0]
    heads = queries_ref.shape[1] // DH
    base = lax.axis_index("ctx") * tokens
    bounds = bounds_of(lengths_ref)
    for block in range(tokens // ROWS):
        count = (block + 1) * ROWS
        rows = slice(block * ROWS, (block + 1) * ROWS)
        bias = bias_of(bounds, base + block * ROWS, ROWS, base, count)
        key, value = own_ref[:count, :], with_ones(own_ref[tokens : tokens + count, :])
        for h in range(heads):
            there = slice(h * ROWS, (h + 1) * ROWS)
            at = slice((block * heads + h) * ROWS, (block * heads + h + 1) * ROWS)
            found = lax.dot_general(
                queries_ref[rows, h * DH : (h + 1) * DH], key, NT, preferred_element_type=F32
            )
            found = found + bias
            scores[there, :count] = found
            top = found[:, :128]
            for p in range(128, count, 128):
                top = jnp.maximum(top, found[:, p : p + 128])
            top = jnp.max(top, axis=1, keepdims=True) * FACTOR + PLACED
            tops_ref[at, :] = jnp.broadcast_to(top, (ROWS, 128))
        for h in range(heads):
            there = slice(h * ROWS, (h + 1) * ROWS)
            at = slice((block * heads + h) * ROWS, (block * heads + h + 1) * ROWS)
            totals_ref[at, :] = jnp.dot(
                weighted(scores[there, :count], tops_ref[at, :]), value, preferred_element_type=F32
            )


def add_piece(bounds, base, block, origin, queries_ref, piece_ref, totals_ref, tops_ref):
    tokens = queries_ref.shape[0]
    heads = queries_ref.shape[1] // DH
    s = base + block * ROWS
    first = origin * tokens
    needed = (first < base) & (first + tokens > doc_start(bounds, s))
    whole = first >= doc_start(bounds, s + ROWS - 1)
    half = first + tokens <= doc_start(bounds, s + ROWS // 2)

    def add(bias, rows):
        key, value = piece_ref[:tokens, :], with_ones(piece_ref[tokens:, :])
        for h in range(heads):
            at = pl.ds(pl.multiple_of((block * heads + h) * ROWS, ROWS), rows)
            query = queries_ref[pl.ds(pl.multiple_of(block * ROWS, ROWS), rows), h * DH : (h + 1) * DH]
            found = lax.dot_general(query, key, NT, preferred_element_type=F32)
            if bias is not None:
                found = found + bias
            totals_ref[at, :] += jnp.dot(weighted(found, tops_ref[at, :]), value, preferred_element_type=F32)

    @pl.when(needed & whole)
    def _():
        add(None, ROWS)

    @pl.when(needed & jnp.logical_not(whole) & jnp.logical_not(half))
    def _():
        add(bias_of(bounds, s, ROWS, first, tokens), ROWS)

    @pl.when(needed & half)
    def _():
        add(bias_of(bounds, s, ROWS // 2, first, tokens), ROWS // 2)


def middle_kernel(count, which, block, lengths_ref, queries_ref, tops_ref, totals_in, *refs):
    pieces, totals_ref = refs[:-1], refs[-1]
    tokens = queries_ref.shape[0]
    base = lax.axis_index("ctx") * tokens
    bounds = bounds_of(lengths_ref)

    for m, piece in zip(which, pieces):
        add_piece(bounds, base, block, origin_of(m, count), queries_ref, piece, totals_ref, tops_ref)


def last_kernel(count, which, lengths_ref, queries_ref, tops_ref, totals_in, *refs):
    pieces, out_ref, totals_ref = refs[:count], refs[count], refs[count + 1]
    tokens = queries_ref.shape[0]
    heads = queries_ref.shape[1] // DH
    base = lax.axis_index("ctx") * tokens
    bounds = bounds_of(lengths_ref)

    def row_block(block, _):
        for m in which:
            add_piece(bounds, base, block, origin_of(m, count), queries_ref, pieces[m], totals_ref, tops_ref)
        return 0

    lax.fori_loop(0, tokens // ROWS, row_block, 0)

    def divided(block, h):
        at = pl.ds(pl.multiple_of((block * heads + h) * ROWS, ROWS), ROWS)
        total = totals_ref[at, DH:]
        return (totals_ref[at, :DH] * pl.reciprocal(total, approx=True)).astype(BF16), total

    highest = jnp.zeros((ROWS, DH), F32)
    for block in range(tokens // ROWS):
        for h in range(heads):
            found, total = divided(block, h)
            out_ref[block * ROWS : (block + 1) * ROWS, h * DH : (h + 1) * DH] = found
            highest = jnp.maximum(highest, total)

    def again(block, h, at):
        s = base + block * ROWS
        rows = pl.ds(pl.multiple_of(block * ROWS, ROWS), ROWS)
        cols = pl.ds(pl.multiple_of(h * DH, DH), DH)
        query = queries_ref[rows, cols]

        def found_of(m):
            found = lax.dot_general(query, pieces[m][:tokens, :], NT, preferred_element_type=F32)
            return found + bias_of(bounds, s, ROWS, origin_of(m, count) * tokens, tokens)

        top = jnp.full((ROWS, 1), LOW, F32)
        for m in range(count):
            top = jnp.maximum(top, jnp.max(found_of(m), axis=1, keepdims=True))
        totals_ref[at, :] = jnp.zeros((ROWS, 2 * DH), F32)
        for m in range(count):
            weights = jnp.exp2((found_of(m) - top) * FACTOR).astype(BF16)
            totals_ref[at, :] += jnp.dot(weights, with_ones(pieces[m][tokens:, :]), preferred_element_type=F32)
        out_ref[rows, cols] = divided(block, h)[0]

    @pl.when(jnp.logical_not(jnp.max(highest) < 2.0**115))
    def _():
        def one(i, _):
            at = pl.ds(pl.multiple_of(i * ROWS, ROWS), ROWS)

            @pl.when(jnp.logical_not(jnp.max(totals_ref[at, DH:]) < 2.0**115))
            def _():
                again(i // heads, i % heads, at)

            return 0

        lax.fori_loop(0, tokens // ROWS * heads, one, 0)


def local(doc_lengths, lin_q, lin_k, lin_v, log_decay, lin_gain, soft_q, soft_k, soft_v):
    doc_lengths = doc_lengths.reshape(1, -1)
    tokens = lin_q.shape[0]
    heads = lin_gain.shape[0] // DH
    count = lax.axis_size("ctx")
    bits = count.bit_length() - 1
    blocks = tokens // BLK

    head_place = lax.axis_index("head")
    own_keys, own_values = soft_k, soft_v
    for bit in range((lax.axis_size("head") // KVH).bit_length() - 1):
        far_keys, far_values = swapped((own_keys, own_values), "head", bit)
        upper = head_place // (1 << bit) % 2 == 1

        def beside(own, far):
            return jnp.where(upper, jnp.concatenate([far, own], axis=1), jnp.concatenate([own, far], axis=1))

        own_keys, own_values = beside(own_keys, far_keys), beside(own_values, far_values)
    own, log_decay, doc_lengths = pl.pallas_call(
        fetch_kernel,
        out_shape=(
            pltpu.VMEM((2 * tokens, DH), BF16),
            pltpu.VMEM(log_decay.shape, F32),
            pltpu.VMEM(doc_lengths.shape, jnp.int32),
        ),
        in_specs=[HBM] * 4,
        out_specs=(VMEM,) * 3,
        scratch_shapes=[pltpu.SemaphoreType.DMA((4,))],
        compiler_params=within(2),
        cost_estimate=lasting(1),
        name="fetch",
    )(in_hbm(own_keys), in_hbm(own_values), in_hbm(log_decay), in_hbm(doc_lengths))
    own, lin_k = lax.optimization_barrier((own, lin_k))
    pieces = [own]
    for bit in range(bits):
        pieces = pieces + [swapped(piece, "ctx", bit) for piece in pieces]
        if bit == 0:
            pieces[1], queries_later = lax.optimization_barrier((pieces[1], lin_q))
            pieces[0], doc_lengths = lax.optimization_barrier((pieces[0], jnp.maximum(doc_lengths, 1)))

    msg_rows = heads * DH + -(-2 * heads // 16) * 16
    msg = jax.ShapeDtypeStruct((msg_rows, DH), BF16)
    total, first, sums = pl.pallas_call(
        states_kernel,
        out_shape=(
            pltpu.VMEM(msg.shape, BF16),
            pltpu.VMEM((max(blocks - 1, 1), heads * DH, DH), BF16),
            pltpu.VMEM(log_decay.shape, F32),
        ),
        in_specs=[VMEM, HBM, HBM, VMEM],
        out_specs=(VMEM,) * 3,
        scratch_shapes=[pltpu.VMEM(lin_k.shape, BF16)] * 2 + [pltpu.SemaphoreType.DMA((2, blocks))],
        cost_estimate=lasting(2.5),
        compiler_params=within(12),
        name="states",
    )(doc_lengths, in_hbm(lin_k), in_hbm(lin_v), log_decay)

    inside, entering = pl.pallas_call(
        inside_kernel,
        out_shape=(pltpu.VMEM(lin_q.shape, BF16), pltpu.VMEM(lin_q.shape, F32)),
        in_specs=[VMEM] + [VMEM] * 4,
        out_specs=(VMEM, VMEM),
        cost_estimate=lasting(4),
        compiler_params=within(12),
        name="inside",
    )(doc_lengths, queries_later, lin_k, lin_v, sums)

    prefix = None
    for bit in range(bits - 1):
        far = swapped(total, "ctx", bit)
        if bit == 0:
            prefix = far
        else:
            prefix = pl.pallas_call(
                functools.partial(prefix_kernel, heads, bit),
                out_shape=msg,
                in_specs=[VMEM] * 2,
                out_specs=VMEM,
                compiler_params=within(8),
        name="prefix",
            )(prefix, far)
        total = pl.pallas_call(
            functools.partial(total_kernel, heads, bit),
            out_shape=msg,
            in_specs=[VMEM] * 2,
            out_specs=VMEM,
            cost_estimate=lasting(1),
            compiler_params=within(8),
        name="total",
        )(total, far)

    totals = jax.ShapeDtypeStruct((heads * tokens, 2 * DH), F32)
    tops = jax.ShapeDtypeStruct((heads * tokens, 128), F32)
    totals, tops = pl.pallas_call(
        near_kernel,
        out_shape=(totals, tops),
        in_specs=[VMEM, VMEM, VMEM],
        out_specs=(VMEM, VMEM),
        scratch_shapes=[pltpu.VMEM((heads * ROWS, tokens), F32)],
        compiler_params=within(20),
        cost_estimate=lasting(4),
        name="near",
    )(doc_lengths, soft_q, pieces[0])
    early = [m for m in range(2, count) if m.bit_count() == 1]
    def middle(block, totals):
        return pl.pallas_call(
            functools.partial(middle_kernel, count, early, block),
            out_shape=jax.ShapeDtypeStruct(totals.shape, F32),
            in_specs=[VMEM] + [VMEM] * (3 + len(early)),
            out_specs=VMEM,
            input_output_aliases={3: 0},
            compiler_params=within(24),
            cost_estimate=lasting(2),
            name="middle",
        )(doc_lengths, soft_q, tops, totals, *[pieces[m] for m in early])

    steps = tokens // ROWS
    for block in range(steps // 2):
        totals = middle(block, totals)
    total, totals = lax.optimization_barrier((total, totals))
    far = swapped(total, "ctx", bits - 1)
    for block in range(steps // 2, steps):
        totals = middle(block, totals)
    late = [m for m in range(1, count) if m not in early]
    soft_out, _ = pl.pallas_call(
        functools.partial(last_kernel, count, late),
        out_shape=(jax.ShapeDtypeStruct(soft_q.shape, BF16), jax.ShapeDtypeStruct(totals.shape, F32)),
        in_specs=[VMEM] + [VMEM] * (3 + count),
        out_specs=(VMEM, VMEM),
        input_output_aliases={3: 1},
        compiler_params=within(24),
        cost_estimate=lasting(4),
        name="last",
    )(doc_lengths, soft_q, tops, totals, *pieces)

    wide = jax.ShapeDtypeStruct(lin_q.shape, BF16)
    return pl.pallas_call(
        functools.partial(across_kernel, bits - 1),
        out_shape=(wide, wide),
        in_specs=[VMEM] * 10,
        out_specs=(HBM, HBM),
        scratch_shapes=[pltpu.VMEM(lin_q.shape, BF16), pltpu.SemaphoreType.DMA((1 + blocks,))],
        compiler_params=within(12),
        cost_estimate=lasting(3),
        name="across",
    )(doc_lengths, lin_q, inside, entering, sums, lin_gain.reshape(1, -1), first, prefix, far, soft_out)


def solution(mesh):
    rows = P("ctx", "head")
    placed = (P(), rows, rows, rows, P("head", "ctx"), P("head"), rows, rows, rows)
    return jax.shard_map(
        local, mesh=mesh, in_specs=placed, out_specs=(rows, rows), check_vma=False
    )
```

```python
import functools

import jax
import jax.numpy as jnp
from jax import lax
from jax.experimental import pallas as pl
from jax.experimental.pallas import tpu as pltpu
from jax.sharding import PartitionSpec as P

KVH = 8
DH = 128
BLK = 256
ROWS = 256
PLACED = 90.0
LOW = -1e30
LOG2E = 1.4426950408889634
FACTOR = LOG2E * DH**-0.5
F32 = jnp.float32
BF16 = jnp.bfloat16
NT = (((1,), (1,)), ((), ()))
TN = (((0,), (0,)), ((), ()))
HBM = pl.BlockSpec(memory_space=pltpu.HBM)
VMEM = pl.BlockSpec(memory_space=pltpu.VMEM)


def within(mib):
    return pltpu.CompilerParams(vmem_limit_bytes=mib * 1024 * 1024)


def in_hbm(array):
    return pltpu.with_memory_space_constraint(array, pltpu.HBM)


def lasting(us):
    return pl.CostEstimate(flops=int(us * 0.8e9), bytes_accessed=0, transcendentals=0)


def swapped(value, axis, bit):
    return lax.ppermute(value, axis, [(i, i ^ 1 << bit) for i in range(lax.axis_size(axis))])


def bounds_of(lengths_ref):
    out, total = [], 0
    lengths = lengths_ref[...]
    for d in range(lengths.shape[1]):
        total = total + lengths[0, d]
        out.append(total)
    return out


def doc_start(bounds, position):
    start = jnp.zeros_like(position)
    for bound in bounds:
        start = jnp.where(bound <= position, bound, start)
    return start


def log_sums(decay):
    rows = lax.broadcasted_iota(jnp.int32, (BLK, BLK), 0)
    cols = lax.broadcasted_iota(jnp.int32, (BLK, BLK), 1)
    upper = jnp.where(rows <= cols, 1.0, 0.0).astype(BF16)
    found = jnp.dot(split(decay, 3).astype(BF16), upper, preferred_element_type=F32)
    count = decay.shape[0]
    return found[:count] + found[count : 2 * count] + found[2 * count :]


def split(value, count):
    terms = []
    for _ in range(count):
        term = value.astype(BF16).astype(F32)
        terms.append(term)
        value = value - term
    return jnp.concatenate(terms, axis=0)


def over_lanes(rows_form, count):
    heads = rows_form.shape[0]
    stacked = split(rows_form, count)
    extra = -stacked.shape[0] % 16
    if extra:
        stacked = jnp.concatenate([stacked, jnp.zeros((extra, stacked.shape[1]), F32)], axis=0)
    depth = stacked.shape[0]
    row = lax.broadcasted_iota(jnp.int32, (depth, heads * DH), 0)
    col = lax.broadcasted_iota(jnp.int32, (depth, heads * DH), 1)
    picks = jnp.where((row % heads == col // DH) & (row < count * heads), 1.0, 0.0).astype(BF16)
    return lax.dot_general(stacked.astype(BF16), picks, TN, preferred_element_type=F32)


def fetch_kernel(keys, values, decay, lengths, own_ref, decay_ref, lengths_ref, sems):
    tokens = keys.shape[0]
    pairs = [
        (keys, own_ref.at[pl.ds(0, tokens), :]),
        (values, own_ref.at[pl.ds(tokens, tokens), :]),
        (decay, decay_ref),
        (lengths, lengths_ref),
    ]
    copies = [pltpu.make_async_copy(a, b, sems.at[i]) for i, (a, b) in enumerate(pairs)]
    for copy in copies:
        copy.start()
    for copy in copies:
        copy.wait()


def states_kernel(lengths_ref, keys_hbm, values_hbm, decay_ref, msg_ref, first_ref, sums_ref, keys_ref, values_ref, sems):
    heads = decay_ref.shape[0]
    tokens = keys_ref.shape[0]
    base = lax.axis_index("ctx") * tokens
    bounds = bounds_of(lengths_ref)
    place = lax.broadcasted_iota(jnp.int32, (1, BLK), 1)
    blocks = tokens // BLK
    copies = []
    for b in range(blocks):
        rows = slice(b * BLK, (b + 1) * BLK)
        copies.append(pltpu.make_async_copy(keys_hbm.at[rows, :], keys_ref.at[rows, :], sems.at[0, b]))
        copies.append(pltpu.make_async_copy(values_hbm.at[rows, :], values_ref.at[rows, :], sems.at[1, b]))
    for copy in copies:
        copy.start()
    through = jnp.ones((heads, 1), F32)
    weights, factors = [], []
    for b in range(blocks):
        s = base + b * BLK
        start_last = doc_start(bounds, s + BLK - 1)
        kept = jnp.where(start_last < s, 1.0, 0.0).astype(F32)
        sums = log_sums(decay_ref[:, b * BLK : (b + 1) * BLK])
        sums_ref[:, b * BLK : (b + 1) * BLK] = sums
        closing = sums[:, BLK - 1 : BLK]
        weight = jnp.where(s + place >= start_last, jnp.exp(closing - sums), 0.0)
        weights.append(over_lanes(weight, 2))
        factors.append(kept * jnp.exp(closing))
        through = through * factors[b]
    state = [None] * heads
    for b in range(blocks):
        copies[2 * b].wait()
        copies[2 * b + 1].wait()
        rows = slice(b * BLK, (b + 1) * BLK)
        for h in range(heads):
            cols = slice(h * DH, (h + 1) * DH)
            weighted = (keys_ref[rows, cols].astype(F32) * weights[b][:, cols]).astype(BF16)
            update = lax.dot_general(weighted, values_ref[rows, cols], TN, preferred_element_type=F32)
            state[h] = update if b == 0 else factors[b][h : h + 1, :] * state[h] + update
            if b < blocks - 1:
                first_ref[b, cols, :] = update.astype(BF16)
    for h in range(heads):
        msg_ref[h * DH : (h + 1) * DH, :] = state[h].astype(BF16)
    tail = jnp.broadcast_to(split(through, 2), (2 * heads, DH))
    extra = msg_ref.shape[0] - heads * DH - 2 * heads
    if extra:
        tail = jnp.concatenate([tail, jnp.zeros((extra, DH), F32)], axis=0)
    msg_ref[heads * DH :, :] = tail.astype(BF16)


def inside_kernel(lengths_ref, queries_ref, keys_ref, values_ref, sums_ref, out_ref, entering_ref):
    heads = sums_ref.shape[0]
    tokens = keys_ref.shape[0]
    base = lax.axis_index("ctx") * tokens
    bounds = bounds_of(lengths_ref)
    rows = lax.broadcasted_iota(jnp.int32, (BLK, BLK), 0)
    cols = lax.broadcasted_iota(jnp.int32, (BLK, BLK), 1)
    place = lax.broadcasted_iota(jnp.int32, (BLK, 1), 0)
    across = lax.broadcasted_iota(jnp.int32, (1, BLK), 1)
    for b in range(tokens // BLK):
        s = base + b * BLK
        start = doc_start(bounds, s + place) - s
        bias = jnp.where((cols <= rows) & (cols >= start), 0.0, LOW)
        here = slice(b * BLK, (b + 1) * BLK)
        sums = sums_ref[:, here] * LOG2E
        down = over_lanes(sums, 3)
        entering = jnp.where(doc_start(bounds, s + across) < s, jnp.exp2(sums), 0.0)
        entering_ref[here, :] = over_lanes(entering, 2)
        for h in range(heads):
            there = slice(h * DH, (h + 1) * DH)
            upright = jnp.concatenate([down[:, there]] * (BLK // DH), axis=1)
            spread = upright - sums[h : h + 1, :] + bias
            scores = lax.dot_general(
                queries_ref[here, there], keys_ref[here, there], NT, preferred_element_type=F32
            )
            scores = (scores * jnp.exp2(spread)).astype(BF16)
            out_ref[here, there] = jnp.dot(
                scores, values_ref[here, there], preferred_element_type=F32
            ).astype(BF16)


def through_of(msg_ref, heads, h):
    high = msg_ref[heads * DH + h : heads * DH + h + 1, :].astype(F32)
    low = msg_ref[heads * DH + heads + h : heads * DH + heads + h + 1, :].astype(F32)
    return high + low


def joined(heads, early_ref, late_ref, swap, out_ref):
    def pick(here):
        one, two = early_ref[here, :].astype(F32), late_ref[here, :].astype(F32)
        return jnp.where(swap, two, one), jnp.where(swap, one, two)

    def through(h):
        high = pick(slice(heads * DH + h, heads * DH + h + 1))
        low = pick(slice(heads * DH + heads + h, heads * DH + heads + h + 1))
        return high[0] + low[0], high[1] + low[1]

    tails = []
    for h in range(heads):
        here = slice(h * DH, (h + 1) * DH)
        early, late = pick(here)
        early_through, late_through = through(h)
        out_ref[here, :] = (late_through * early + late).astype(BF16)
        tails.append(late_through * early_through)
    tail = jnp.concatenate(tails, axis=0)
    high = tail.astype(BF16).astype(F32)
    pieces = [high, tail - high]
    extra = out_ref.shape[0] - heads * DH - 2 * heads
    if extra:
        pieces.append(jnp.zeros((extra, DH), F32))
    out_ref[heads * DH :, :] = jnp.concatenate(pieces, axis=0).astype(BF16)


def upper_half(bit):
    return (lax.axis_index("ctx") // (1 << bit)) % 2 == 1


def total_kernel(heads, bit, total_ref, far_ref, new_total_ref):
    joined(heads, total_ref, far_ref, upper_half(bit), new_total_ref)


def prefix_kernel(heads, bit, prefix_ref, far_ref, new_prefix_ref):
    if bit == 1:
        first = jnp.where(upper_half(0), 1.0, 0.0).astype(F32)
        rows = prefix_ref.shape[0]
        tail = lax.broadcasted_iota(jnp.int32, (rows, DH), 0) - heads * DH
        own = prefix_ref[...].astype(F32) * first
        neutral = jnp.where((tail >= 0) & (tail < heads), 1.0 - first, 0.0)
        prefix_ref = (own + neutral).astype(BF16)

    @pl.when(upper_half(bit))
    def _():
        joined(heads, far_ref, prefix_ref, False, new_prefix_ref)

    @pl.when(jnp.logical_not(upper_half(bit)))
    def _():
        new_prefix_ref[...] = prefix_ref[...]


def across_kernel(
    bit, lengths_ref, queries_ref, inside_ref, entering_ref, sums_ref, gain_ref, first_ref, prefix_ref, far_ref, soft_ref,
    out_hbm, soft_hbm, out_ref, sems,
):
    soft_copy = pltpu.make_async_copy(soft_ref, soft_hbm, sems.at[0])
    soft_copy.start()
    copies = []
    heads = sums_ref.shape[0]
    tokens = queries_ref.shape[0]
    place_ctx = lax.axis_index("ctx")
    base = place_ctx * tokens
    upper = jnp.where(upper_half(bit), 1.0, 0.0).astype(F32)
    valid = jnp.where(upper_half(0), 1.0, 0.0).astype(F32) if bit == 1 else 1.0
    bounds = bounds_of(lengths_ref)
    state = []
    for h in range(heads):
        here = slice(h * DH, (h + 1) * DH)
        through = upper * (valid * through_of(prefix_ref, heads, h) + (1.0 - valid))
        state.append(valid * prefix_ref[here, :].astype(F32) + through * far_ref[here, :].astype(F32))
    pair = 2 * DH
    row = lax.broadcasted_iota(jnp.int32, (pair, pair), 0)
    col = lax.broadcasted_iota(jnp.int32, (pair, pair), 1)
    ones = jnp.where(row // DH == col // DH, 1.0, 0.0).astype(BF16)
    zeros = jnp.zeros((DH, DH), BF16)
    for b in range(tokens // BLK):
        s = base + b * BLK
        here = slice(b * BLK, (b + 1) * BLK)
        start_last = doc_start(bounds, s + BLK - 1)
        kept = jnp.where(start_last < s, 1.0, 0.0).astype(F32)
        factor = kept * jnp.exp(sums_ref[:, (b + 1) * BLK - 1 : (b + 1) * BLK])
        for h in range(0, heads, 2):
            there = slice(h * DH, (h + 2) * DH)
            left = jnp.concatenate([state[h].astype(BF16), zeros], axis=1)
            right = jnp.concatenate([zeros, state[h + 1].astype(BF16)], axis=1)
            across = jnp.dot(
                queries_ref[here, there],
                jnp.concatenate([left, right], axis=0),
                preferred_element_type=F32,
            )
            raw = inside_ref[here, there].astype(F32) + across * entering_ref[here, there]
            square = jnp.dot((raw * raw).astype(BF16), ones, preferred_element_type=F32)
            scale = lax.rsqrt(square * (1.0 / DH) + 1e-06)
            out_ref[here, there] = (raw * scale * gain_ref[:, there]).astype(BF16)
            sem = sems.at[1 + len(copies)]
            copies.append(pltpu.make_async_copy(out_ref.at[here, there], out_hbm.at[here, there], sem))
            copies[-1].start()
            if b < tokens // BLK - 1:
                for one in (h, h + 1):
                    update = first_ref[b, one * DH : (one + 1) * DH, :].astype(F32)
                    state[one] = factor[one : one + 1, :] * state[one] + update
    soft_copy.wait()
    for copy in copies:
        copy.wait()


def origin_of(m, count):
    place = lax.axis_index("ctx")
    origin = jnp.int32(0)
    bit = 1
    while bit < count:
        mine = (place // bit) % 2
        origin = origin + bit * (1 - mine if m & bit else mine)
        bit *= 2
    return origin


def bias_of(bounds, first_row, rows, first_key, count):
    row = first_row + lax.broadcasted_iota(jnp.int32, (rows, 1), 0)
    key = first_key + lax.broadcasted_iota(jnp.int32, (rows, count), 1)
    return jnp.where((key >= doc_start(bounds, row)) & (key <= row), 0.0, LOW)


def with_ones(values):
    return jnp.concatenate([values, jnp.ones(values.shape, BF16)], axis=1)


def weighted(found, top):
    spread = [found[:, p : p + 128] * FACTOR - top for p in range(0, found.shape[1], 128)]
    return jnp.concatenate([jnp.exp2(x).astype(BF16) for x in spread], axis=1)


def near_kernel(lengths_ref, queries_ref, own_ref, totals_ref, tops_ref, scores):
    tokens = queries_ref.shape[0]
    heads = queries_ref.shape[1] // DH
    base = lax.axis_index("ctx") * tokens
    bounds = bounds_of(lengths_ref)
    for block in range(tokens // ROWS):
        count = (block + 1) * ROWS
        rows = slice(block * ROWS, (block + 1) * ROWS)
        bias = bias_of(bounds, base + block * ROWS, ROWS, base, count)
        key, value = own_ref[:count, :], with_ones(own_ref[tokens : tokens + count, :])
        for h in range(heads):
            there = slice(h * ROWS, (h + 1) * ROWS)
            at = slice((block * heads + h) * ROWS, (block * heads + h + 1) * ROWS)
            found = lax.dot_general(
                queries_ref[rows, h * DH : (h + 1) * DH], key, NT, preferred_element_type=F32
            )
            found = found + bias
            scores[there, :count] = found
            top = found[:, :128]
            for p in range(128, count, 128):
                top = jnp.maximum(top, found[:, p : p + 128])
            top = jnp.max(top, axis=1, keepdims=True) * FACTOR + PLACED
            tops_ref[at, :] = jnp.broadcast_to(top, (ROWS, 128))
        for h in range(heads):
            there = slice(h * ROWS, (h + 1) * ROWS)
            at = slice((block * heads + h) * ROWS, (block * heads + h + 1) * ROWS)
            totals_ref[at, :] = jnp.dot(
                weighted(scores[there, :count], tops_ref[at, :]), value, preferred_element_type=F32
            )


def add_piece(bounds, base, block, origin, queries_ref, piece_ref, totals_ref, tops_ref):
    tokens = queries_ref.shape[0]
    heads = queries_ref.shape[1] // DH
    s = base + block * ROWS
    first = origin * tokens
    needed = (first < base) & (first + tokens > doc_start(bounds, s))
    whole = first >= doc_start(bounds, s + ROWS - 1)
    half = first + tokens <= doc_start(bounds, s + ROWS // 2)

    def add(bias, rows):
        key, value = piece_ref[:tokens, :], with_ones(piece_ref[tokens:, :])
        for h in range(heads):
            at = pl.ds(pl.multiple_of((block * heads + h) * ROWS, ROWS), rows)
            query = queries_ref[pl.ds(pl.multiple_of(block * ROWS, ROWS), rows), h * DH : (h + 1) * DH]
            found = lax.dot_general(query, key, NT, preferred_element_type=F32)
            if bias is not None:
                found = found + bias
            totals_ref[at, :] += jnp.dot(weighted(found, tops_ref[at, :]), value, preferred_element_type=F32)

    @pl.when(needed & whole)
    def _():
        add(None, ROWS)

    @pl.when(needed & jnp.logical_not(whole) & jnp.logical_not(half))
    def _():
        add(bias_of(bounds, s, ROWS, first, tokens), ROWS)

    @pl.when(needed & half)
    def _():
        add(bias_of(bounds, s, ROWS // 2, first, tokens), ROWS // 2)


def middle_kernel(count, which, block, lengths_ref, queries_ref, tops_ref, totals_in, *refs):
    pieces, totals_ref = refs[:-1], refs[-1]
    tokens = queries_ref.shape[0]
    base = lax.axis_index("ctx") * tokens
    bounds = bounds_of(lengths_ref)

    for m, piece in zip(which, pieces):
        add_piece(bounds, base, block, origin_of(m, count), queries_ref, piece, totals_ref, tops_ref)


def last_kernel(count, which, lengths_ref, queries_ref, tops_ref, totals_in, *refs):
    pieces, out_ref, totals_ref = refs[:count], refs[count], refs[count + 1]
    tokens = queries_ref.shape[0]
    heads = queries_ref.shape[1] // DH
    base = lax.axis_index("ctx") * tokens
    bounds = bounds_of(lengths_ref)

    def row_block(block, _):
        for m in which:
            add_piece(bounds, base, block, origin_of(m, count), queries_ref, pieces[m], totals_ref, tops_ref)
        return 0

    lax.fori_loop(0, tokens // ROWS, row_block, 0)

    def divided(block, h):
        at = pl.ds(pl.multiple_of((block * heads + h) * ROWS, ROWS), ROWS)
        total = totals_ref[at, DH:]
        return (totals_ref[at, :DH] * pl.reciprocal(total, approx=True)).astype(BF16), total

    highest = jnp.zeros((ROWS, DH), F32)
    for block in range(tokens // ROWS):
        for h in range(heads):
            found, total = divided(block, h)
            out_ref[block * ROWS : (block + 1) * ROWS, h * DH : (h + 1) * DH] = found
            highest = jnp.maximum(highest, total)

    def again(block, h, at):
        s = base + block * ROWS
        rows = pl.ds(pl.multiple_of(block * ROWS, ROWS), ROWS)
        cols = pl.ds(pl.multiple_of(h * DH, DH), DH)
        query = queries_ref[rows, cols]

        def found_of(m):
            found = lax.dot_general(query, pieces[m][:tokens, :], NT, preferred_element_type=F32)
            return found + bias_of(bounds, s, ROWS, origin_of(m, count) * tokens, tokens)

        top = jnp.full((ROWS, 1), LOW, F32)
        for m in range(count):
            top = jnp.maximum(top, jnp.max(found_of(m), axis=1, keepdims=True))
        totals_ref[at, :] = jnp.zeros((ROWS, 2 * DH), F32)
        for m in range(count):
            weights = jnp.exp2((found_of(m) - top) * FACTOR).astype(BF16)
            totals_ref[at, :] += jnp.dot(weights, with_ones(pieces[m][tokens:, :]), preferred_element_type=F32)
        out_ref[rows, cols] = divided(block, h)[0]

    @pl.when(jnp.logical_not(jnp.max(highest) < 2.0**115))
    def _():
        def one(i, _):
            at = pl.ds(pl.multiple_of(i * ROWS, ROWS), ROWS)

            @pl.when(jnp.logical_not(jnp.max(totals_ref[at, DH:]) < 2.0**115))
            def _():
                again(i // heads, i % heads, at)

            return 0

        lax.fori_loop(0, tokens // ROWS * heads, one, 0)


def local(doc_lengths, lin_q, lin_k, lin_v, log_decay, lin_gain, soft_q, soft_k, soft_v):
    doc_lengths = doc_lengths.reshape(1, -1)
    tokens = lin_q.shape[0]
    heads = lin_gain.shape[0] // DH
    count = lax.axis_size("ctx")
    bits = count.bit_length() - 1
    blocks = tokens // BLK

    head_place = lax.axis_index("head")
    own_keys, own_values = soft_k, soft_v
    for bit in range((lax.axis_size("head") // KVH).bit_length() - 1):
        far_keys, far_values = swapped((own_keys, own_values), "head", bit)
        upper = head_place // (1 << bit) % 2 == 1

        def beside(own, far):
            return jnp.where(upper, jnp.concatenate([far, own], axis=1), jnp.concatenate([own, far], axis=1))

        own_keys, own_values = beside(own_keys, far_keys), beside(own_values, far_values)
    own, log_decay, doc_lengths = pl.pallas_call(
        fetch_kernel,
        out_shape=(
            pltpu.VMEM((2 * tokens, DH), BF16),
            pltpu.VMEM(log_decay.shape, F32),
            pltpu.VMEM(doc_lengths.shape, jnp.int32),
        ),
        in_specs=[HBM] * 4,
        out_specs=(VMEM,) * 3,
        scratch_shapes=[pltpu.SemaphoreType.DMA((4,))],
        compiler_params=within(2),
        cost_estimate=lasting(1),
        name="fetch",
    )(in_hbm(own_keys), in_hbm(own_values), in_hbm(log_decay), in_hbm(doc_lengths))
    own, lin_k = lax.optimization_barrier((own, lin_k))
    pieces = [own]
    for bit in range(bits):
        pieces = pieces + [swapped(piece, "ctx", bit) for piece in pieces]
        if bit == 0:
            pieces[1], queries_later = lax.optimization_barrier((pieces[1], lin_q))
            pieces[0], doc_lengths = lax.optimization_barrier((pieces[0], jnp.maximum(doc_lengths, 1)))

    msg_rows = heads * DH + -(-2 * heads // 16) * 16
    msg = jax.ShapeDtypeStruct((msg_rows, DH), BF16)
    total, first, sums = pl.pallas_call(
        states_kernel,
        out_shape=(
            pltpu.VMEM(msg.shape, BF16),
            pltpu.VMEM((max(blocks - 1, 1), heads * DH, DH), BF16),
            pltpu.VMEM(log_decay.shape, F32),
        ),
        in_specs=[VMEM, HBM, HBM, VMEM],
        out_specs=(VMEM,) * 3,
        scratch_shapes=[pltpu.VMEM(lin_k.shape, BF16)] * 2 + [pltpu.SemaphoreType.DMA((2, blocks))],
        cost_estimate=lasting(2.5),
        compiler_params=within(12),
        name="states",
    )(doc_lengths, in_hbm(lin_k), in_hbm(lin_v), log_decay)

    inside, entering = pl.pallas_call(
        inside_kernel,
        out_shape=(pltpu.VMEM(lin_q.shape, BF16), pltpu.VMEM(lin_q.shape, F32)),
        in_specs=[VMEM] + [VMEM] * 4,
        out_specs=(VMEM, VMEM),
        cost_estimate=lasting(4),
        compiler_params=within(12),
        name="inside",
    )(doc_lengths, queries_later, lin_k, lin_v, sums)

    prefix = None
    for bit in range(bits - 1):
        far = swapped(total, "ctx", bit)
        if bit == 0:
            prefix = far
        else:
            prefix = pl.pallas_call(
                functools.partial(prefix_kernel, heads, bit),
                out_shape=msg,
                in_specs=[VMEM] * 2,
                out_specs=VMEM,
                compiler_params=within(8),
        name="prefix",
            )(prefix, far)
        total = pl.pallas_call(
            functools.partial(total_kernel, heads, bit),
            out_shape=msg,
            in_specs=[VMEM] * 2,
            out_specs=VMEM,
            cost_estimate=lasting(1),
            compiler_params=within(8),
        name="total",
        )(total, far)

    totals = jax.ShapeDtypeStruct((heads * tokens, 2 * DH), F32)
    tops = jax.ShapeDtypeStruct((heads * tokens, 128), F32)
    totals, tops = pl.pallas_call(
        near_kernel,
        out_shape=(totals, tops),
        in_specs=[VMEM, VMEM, VMEM],
        out_specs=(VMEM, VMEM),
        scratch_shapes=[pltpu.VMEM((heads * ROWS, tokens), F32)],
        compiler_params=within(20),
        cost_estimate=lasting(4),
        name="near",
    )(doc_lengths, soft_q, pieces[0])
    early = [m for m in range(2, count) if m.bit_count() == 1]
    def middle(block, totals):
        return pl.pallas_call(
            functools.partial(middle_kernel, count, early, block),
            out_shape=jax.ShapeDtypeStruct(totals.shape, F32),
            in_specs=[VMEM] + [VMEM] * (3 + len(early)),
            out_specs=VMEM,
            input_output_aliases={3: 0},
            compiler_params=within(24),
            cost_estimate=lasting(2),
            name="middle",
        )(doc_lengths, soft_q, tops, totals, *[pieces[m] for m in early])

    steps = tokens // ROWS
    for block in range(steps // 2):
        totals = middle(block, totals)
    total, totals = lax.optimization_barrier((total, totals))
    far = swapped(total, "ctx", bits - 1)
    for block in range(steps // 2, steps):
        totals = middle(block, totals)
    late = [m for m in range(1, count) if m not in early]
    soft_out, _ = pl.pallas_call(
        functools.partial(last_kernel, count, late),
        out_shape=(jax.ShapeDtypeStruct(soft_q.shape, BF16), jax.ShapeDtypeStruct(totals.shape, F32)),
        in_specs=[VMEM] + [VMEM] * (3 + count),
        out_specs=(VMEM, VMEM),
        input_output_aliases={3: 1},
        compiler_params=within(24),
        cost_estimate=lasting(4),
        name="last",
    )(doc_lengths, soft_q, tops, totals, *pieces)

    wide = jax.ShapeDtypeStruct(lin_q.shape, BF16)
    return pl.pallas_call(
        functools.partial(across_kernel, bits - 1),
        out_shape=(wide, wide),
        in_specs=[VMEM] * 10,
        out_specs=(HBM, HBM),
        scratch_shapes=[pltpu.VMEM(lin_q.shape, BF16), pltpu.SemaphoreType.DMA((1 + blocks * heads // 2,))],
        compiler_params=within(12),
        cost_estimate=lasting(3),
        name="across",
    )(doc_lengths, lin_q, inside, entering, sums, lin_gain.reshape(1, -1), first, prefix, far, soft_out)


def solution(mesh):
    rows = P("ctx", "head")
    placed = (P(), rows, rows, rows, P("head", "ctx"), P("head"), rows, rows, rows)
    return jax.shard_map(
        local, mesh=mesh, in_specs=placed, out_specs=(rows, rows), check_vma=False
    )
```
